32 devices in a mesh: dp: 2 (over x), expert: 16 (over z, y, core).
Axes of the slice: x: 2, y: 2, z: 4, core: 2. Of those that a mesh axis runs over, the one named last changes fastest.
Arguments:
- query: bfloat16 [32, 2048], P('dp'), may hold values from -1200 to 1200
- new_kv: bfloat16 [32, 1024], P('dp'), may hold values from -5 to 5
- kv_cache: bfloat16 [32, 256, 1024], P('dp', 'expert'), may hold values from -6 to 6
- lengths: int32 [32], P('dp'), may hold values from 2 to 256, as said below
- fork_parent: int32 [4], replicated, may hold values from 0 to 31, as said below
- fork_child: int32 [4], replicated, may hold values from 0 to 30, as said below
- fork_block: int32 [4], replicated, may hold values from 0 to 15, as said below
- out_weight: bfloat16 [2048, 4096], P('expert'), may hold values from -1 to 1
- residual: bfloat16 [32, 4096], P('dp'), may hold values from -300 to 300
- route_ids: int32 [32, 8], replicated, may hold values from 0 to 15, all different within a row; in each aligned block of 16 rows (0 to 15, 16 to 31, ...) at most 16 rows name the same one
- route_weights: float32 [32, 8], replicated, may hold values from 0.02 to 0.3
- w_gate: bfloat16 [16, 4096, 1024], P('expert', None, 'dp'), may hold values from -0.09375 to 0.09375
- w_up: bfloat16 [16, 4096, 1024], P('expert', None, 'dp'), may hold values from -0.09375 to 0.09375
- w_down: bfloat16 [16, 1024, 4096], P('expert', 'dp'), may hold values from -0.1875 to 0.1875
Outputs:
- attn_proj: bfloat16 [32, 4096], P('dp', 'expert')
- expert_mix: bfloat16 [32, 4096], P('dp', 'expert')
The draws below stay inside these ranges and needn't reach their ends.
Inputs may be any that keep to these rules, and one draw needn't show every extreme that they name: `lengths`: at least 2; a fork's child has its parent's length. `fork_parent`: fork g * 2 + d takes its parent from the branches g * 16 to (g + 1) * 16 - 1 and its child from d * 16 to (d + 1) * 16 - 1; parents are distinct, children are distinct, and no child is a parent. `fork_child`: see fork_parent. `fork_block`: at most the block that holds the parent's last cached position, (lengths - 1) // 16. `route_ids`: in each aligned block of 16 rows no expert is named by more than 16 rows, a bound that some block reaches.
All inputs are finite; a program needn't handle non-finite values.
Results may differ from the reference program's by a relative error of at most 0.024.
Values may be sent and summed in bfloat16 or wider, within the bound.
A program may use at most 128 MiB of HBM per device.

```python
import math
import jax
import jax.numpy as jnp
import numpy as np
from jax import lax

D = 4096
HD = 128
KVH = 4
HEADS = 16
EXPERTS = 16
FF = 1024
TOP = 8
BR_GRP = 16
CTX_DEV = 16
B = 32
CTX = 256
KVW = 1024
QW = 2048
CAP = 16
FORKS = 4


def swap_into(row, value, place):
    where_now = jnp.sum(jnp.where(row == value, jnp.arange(row.shape[0], dtype=jnp.int32), 0)).astype(jnp.int32)
    held = row[place]
    return row.at[where_now].set(held).at[place].set(value)


def fork_plan(key):
    plan_key = jax.random.fold_in(key, 11)
    groups = B // BR_GRP

    def shuffle(subkey):
        return jax.random.permutation(subkey, BR_GRP)
    orders = jax.vmap(shuffle)(jax.random.split(plan_key, groups)).astype(jnp.int32)
    last_row = swap_into(orders[groups - 1], BR_GRP - 1, 0)
    last_row = swap_into(last_row, BR_GRP - 2, groups)
    orders = orders.at[groups - 1].set(last_row.astype(jnp.int32))
    group_start = jnp.arange(groups, dtype=jnp.int32) * BR_GRP
    parent = (group_start[:, None] + orders[:, :groups]).reshape(-1).astype(jnp.int32)
    child = (group_start[None, :] + orders[:, groups:2 * groups].T).reshape(-1).astype(jnp.int32)
    drawn = jax.random.randint(jax.random.fold_in(plan_key, 1), (B,), 2, CTX + 1, jnp.int32)
    drawn = drawn.at[parent[0]].set(CTX)
    lengths = drawn.at[child].set(drawn[parent])
    last_block = (lengths[parent] - 1) // CTX_DEV
    fork_at = jax.random.randint(jax.random.fold_in(plan_key, 2), (FORKS,), 0, 1 << 20, jnp.int32) % (last_block + 1)
    fork_at = fork_at.at[0].set(last_block[0])
    return (lengths.astype(jnp.int32), parent, child, fork_at.astype(jnp.int32))


def draw_lengths(key, part):
    return fork_plan(key)[0]


def draw_fork_parent(key, part):
    return fork_plan(key)[1]


def draw_fork_child(key, part):
    return fork_plan(key)[2]


def draw_fork_block(key, part):
    return fork_plan(key)[3]


def first_keys(key):
    return jnp.clip(jax.random.normal(jax.random.fold_in(key, 23), (B, KVH * HD), jnp.float32), -4.0, 4.0)


def draw_kv_cache(key, part):
    shape = (B, CTX, KVW)
    cache = jnp.clip(jax.random.normal(jax.random.fold_in(key, 5), shape, jnp.float32), -6.0, 6.0)
    leading = first_keys(key)
    cache = cache.at[:, 0, :KVH * HD].set(leading)
    return cache.astype(jnp.bfloat16)


def draw_query(key, part):
    shape = (B, QW)
    entries = jnp.clip(jax.random.normal(jax.random.fold_in(key, 3), shape, jnp.float32), -6.0, 6.0)
    return entries.astype(jnp.bfloat16)


def draw_residual(key, part):
    shape = (B, D)
    row_scale = 10.0 ** jax.random.uniform(jax.random.fold_in(key, 9), (B, 1), jnp.float32, 0.0, 0.6)
    column_pos = jnp.arange(D, dtype=jnp.float32)[None, :] / D
    base_values = jnp.clip(jax.random.normal(jax.random.fold_in(key, 8), shape, jnp.float32), -5.0, 5.0)
    column_scale = 10.0 ** column_pos
    return (base_values * row_scale * column_scale).astype(jnp.bfloat16)


def levels(key, dims, cuts, smallest, largest):
    gain = 1.0
    for axis_at, parts in cuts:
        heights = jax.random.uniform(jax.random.fold_in(jax.random.fold_in(key, 6), axis_at), (parts,), jnp.float32, smallest / len(cuts), largest / len(cuts))
        gain = gain * jnp.repeat(jnp.exp(heights), dims[axis_at] // parts).reshape((-1,) + (1,) * (len(dims) - 1 - axis_at))
    return gain


def shared_out(rng, own, number, rows, number_of, top, limit, lean):
    ranking = jax.random.permutation(rng, number_of)
    heavy_load, ordinary = shares(number_of, rows * top, limit, lean, True), shares(number_of, rows * top, limit, lean, False)
    places = jnp.arange(number_of)

    def named(sizes, rotation):
        used = int((sizes > 0).sum())
        fixed = max(1, used // 4)
        moved = fixed + (places - fixed + rotation * (used - fixed)) % max(1, number_of - fixed)
        return jnp.zeros((number_of,), jnp.int32).at[ranking[jnp.where(places < fixed, places, moved)]].set(jnp.asarray(sizes, jnp.int32))

    sizes = jnp.where(number % 4 == 0, named(heavy_load, number // 4), named(ordinary, number - number // 4 - 1))
    mixed = jax.random.permutation(jax.random.fold_in(own, 3), number_of)
    source_of, sink = mixed[0:number_of // 2 * 2:2], mixed[1:number_of // 2 * 2:2]
    slack = jnp.minimum(sizes[source_of] - 1, limit - sizes[sink]) // 2
    slack = jnp.where((source_of == ranking[0]) | (sink == ranking[0]) | (sizes[sink] == 0), 0, jnp.maximum(slack, 0))
    moved = jax.random.randint(jax.random.fold_in(own, 4), (number_of // 2,), 0, 1 << 20) % (slack + 1)
    sizes = sizes.at[source_of].add(-moved).at[sink].add(moved)
    labels = jnp.searchsorted(jnp.cumsum(sizes), jnp.arange(rows * top), side="right").astype(jnp.int32)
    table = labels.reshape(top, rows).T
    table = table[jax.random.permutation(jax.random.fold_in(own, 1), rows)]
    rotation = jax.random.randint(jax.random.fold_in(own, 2), (rows, 1), 0, top)
    return jnp.take_along_axis(table, (jnp.arange(top)[None, :] + rotation) % top, axis=1)


def shares(count, total, reach, skew, full):
    weights = [(1 << 20) // math.isqrt(grade ** skew) + 1 for grade in range(1, count + 1)]
    largest = reach if full else min(reach, max(-(-total // count), total * weights[0] // sum(weights)))
    least = 1 if total - largest >= count - 1 else 0
    counts, spare = [largest] + [least] * (count - 1), total - largest - least * (count - 1)
    while spare > 0:
        candidates = [i for i in range(1, count) if counts[i] < largest] or [i for i in range(1, count) if counts[i] < reach]
        whole, left = sum([weights[i] for i in candidates]), spare
        for i in candidates:
            more = min(reach - counts[i], max(1, left * weights[i] // whole), spare)
            counts[i] = counts[i] + more
            spare = spare - more
    return np.array(counts)


def bell_draw(rng, shape, spread, reach, pieces=(), held_as=jnp.bfloat16):
    array = jax.random.normal(rng, shape, jnp.float32) * spread
    if len(pieces) > 0:
        array = levels(rng, shape, pieces, -0.22, 0.18) * array
    return jnp.clip(array, min=-reach, max=reach).astype(held_as)


def setup_inputs(seed: int = 0) -> dict:
    seeds = jax.random.split(jax.random.key(seed), 15)
    query = draw_query(jax.random.fold_in(seeds[14], 71), 0)
    new_kv = bell_draw(seeds[1], (B, KVW), 1.0, 5.0, ((0, 2),))
    kv_cache = draw_kv_cache(jax.random.fold_in(seeds[14], 71), 0)
    lengths = draw_lengths(jax.random.fold_in(seeds[14], 71), 0)
    fork_parent = draw_fork_parent(jax.random.fold_in(seeds[14], 71), 0)
    fork_child = draw_fork_child(jax.random.fold_in(seeds[14], 71), 0)
    fork_block = draw_fork_block(jax.random.fold_in(seeds[14], 71), 0)
    out_weight = bell_draw(seeds[7], (QW, D), (HD // 4) ** -0.5, 1.0, ((0, 16),))
    residual = draw_residual(jax.random.fold_in(seeds[14], 71), 0)
    route_ids_keys = jax.random.split(jax.random.fold_in(seeds[9], 1), B // BR_GRP)
    route_ids_turns = jax.random.permutation(jax.random.fold_in(seeds[9], 3), B // BR_GRP)
    route_ids = jax.vmap(lambda own, number: shared_out(jax.random.fold_in(seeds[9], 2), own, number, BR_GRP, EXPERTS, TOP, CAP, 2))(route_ids_keys, route_ids_turns).reshape((B, TOP))
    route_weights = jnp.clip(jnp.exp(jax.random.uniform(seeds[10], (B, TOP), jnp.float32, math.log(0.02), math.log(0.3))), 0.02, 0.3)
    w_gate = bell_draw(seeds[11], (EXPERTS, D, FF), D ** -0.5, 0.09375, ((0, 16), (2, 2)))
    w_up = bell_draw(seeds[12], (EXPERTS, D, FF), D ** -0.5, 0.09375, ((0, 16), (2, 2)))
    w_down = bell_draw(seeds[13], (EXPERTS, FF, D), FF ** -0.5, 0.1875, ((0, 16), (1, 2)))
    return {"query": query, "new_kv": new_kv, "kv_cache": kv_cache, "lengths": lengths, "fork_parent": fork_parent, "fork_child": fork_child, "fork_block": fork_block, "out_weight": out_weight, "residual": residual, "route_ids": route_ids, "route_weights": route_weights, "w_gate": w_gate, "w_up": w_up, "w_down": w_down}


def attend_branch(row_items):
    query_row, new_row, cache_rows, length = row_items
    grouping = HEADS // KVH
    key_width = KVH * HD
    score_scale = 1.0 / math.sqrt(HD)
    grouped = query_row.astype(jnp.float32).reshape(KVH, grouping, HD)
    cached_keys = cache_rows[:, :key_width].astype(jnp.float32).reshape(CTX, KVH, HD)
    cached_values = cache_rows[:, key_width:].astype(jnp.float32).reshape(CTX, KVH, HD)
    new_key = new_row[:key_width].astype(jnp.float32).reshape(KVH, HD)
    new_value = new_row[key_width:].astype(jnp.float32).reshape(KVH, HD)
    scores = jnp.einsum('kgd,pkd->kgp', grouped, cached_keys) * score_scale
    own_score = jnp.einsum('kgd,kd->kg', grouped, new_key) * score_scale
    visible = jnp.arange(CTX, dtype=jnp.int32) < length
    scores = jnp.where(visible[None, None, :], scores, -jnp.inf)
    highest = jnp.maximum(lax.optimization_barrier(jnp.max(scores, axis=-1)), own_score)
    weights = jnp.exp(scores - highest[..., None])
    own_weight = jnp.exp(own_score - highest)
    weight_sum = lax.optimization_barrier(jnp.sum(weights, axis=-1)) + own_weight
    rounded = lax.optimization_barrier(weights.astype(jnp.bfloat16)).astype(jnp.float32)
    own_rounded = lax.optimization_barrier(own_weight.astype(jnp.bfloat16)).astype(jnp.float32)
    gathered = jnp.einsum('kgp,pkd->kgd', rounded, cached_values)
    gathered = gathered + own_rounded[..., None] * new_value[:, None, :]
    return (gathered / weight_sum[..., None]).reshape(-1).astype(jnp.bfloat16)

def reference(query, new_kv, kv_cache, lengths, fork_parent, fork_child, fork_block, out_weight, residual, route_ids, route_weights, w_gate, w_up, w_down):
    positions = jnp.arange(CTX, dtype=jnp.int32)
    starts = fork_block * CTX_DEV
    beyond = positions[None, :] >= starts[:, None]
    copied = jnp.where(beyond[:, :, None], kv_cache[fork_parent], kv_cache[fork_child])
    forked_cache = kv_cache.at[fork_child].set(copied)
    heads_out = lax.map(attend_branch, (query, new_kv, forked_cache, lengths))
    projected = jnp.dot(heads_out, out_weight, preferred_element_type=jnp.float32)
    attn_proj = projected.astype(jnp.bfloat16)
    stream = residual.astype(jnp.float32) + projected
    normed = (stream * lax.rsqrt(lax.optimization_barrier(jnp.mean(stream * stream, axis=1, keepdims=True)) + 1e-06)).astype(jnp.bfloat16)

    def expert_token(token_items):
        token_row, expert_ids, gate_values = token_items
        gate_mats = w_gate[expert_ids].astype(jnp.float32)
        up_mats = w_up[expert_ids].astype(jnp.float32)
        down_mats = w_down[expert_ids].astype(jnp.float32)
        row_wide = token_row.astype(jnp.float32)
        gate_proj = jnp.einsum('d,kdf->kf', row_wide, gate_mats)
        up_proj = jnp.einsum('d,kdf->kf', row_wide, up_mats)
        hidden = (jax.nn.silu(gate_proj) * up_proj).astype(jnp.bfloat16)
        expert_out = jnp.einsum('kf,kfd->kd', hidden.astype(jnp.float32), down_mats)
        return lax.optimization_barrier(jnp.sum(gate_values[:, None] * expert_out, axis=0)).astype(jnp.bfloat16)
    expert_mix = lax.map(expert_token, (normed, route_ids, route_weights))
    return (attn_proj, expert_mix)
```

```python
import functools
import math

import jax
import jax.numpy as jnp
from jax import lax
from jax.experimental import pallas as pl
from jax.experimental.pallas import tpu as pltpu
from jax.sharding import PartitionSpec as P

HD = 128
KVH = 4
MESH = pl.DeviceIdType.MESH
F32 = jnp.float32
BF16 = jnp.bfloat16
HIDDEN_SCORE = -1e30


def layer(
    groups,
    owners,
    slice_residual,
    lengths,
    fork_parent,
    fork_child,
    fork_block,
    query,
    new_kv,
    kv_cache,
    residual,
    route_ids,
    route_weights,
    out_weight,
    w_gate,
    w_up,
    w_down,
    attn_out,
    mix_out,
    cache,
    out_held,
    gate_held,
    up_held,
    down_held,
    fork_send,
    fork_recv,
    part_send,
    part_recv,
    proj_send,
    proj_recv,
    stream,
    mix_send,
    mix_recv,
    load_sem,
    fork_send_sem,
    fork_recv_sem,
    part_sem,
    proj_sem,
    stream_send_sem,
    stream_recv_sem,
    mix_sem,
):
    group = lax.axis_index("dp")
    owner = lax.axis_index("expert")
    devices = groups * owners
    rows = query.shape[0]
    positions_dev = kv_cache.shape[1]
    key_width = KVH * HD
    grouping = query.shape[1] // HD // KVH
    width = w_gate.shape[1]
    columns = width // owners
    fork_groups = math.isqrt(fork_parent.shape[0])
    held_groups = fork_groups // groups
    pairs = [(i, k) for i in range(held_groups) for k in range(held_groups)]

    barrier = pltpu.get_barrier_semaphore()

    def greet(step, carry):
        place = lax.rem(group * owners + owner + step, devices)
        pl.semaphore_signal(
            barrier,
            inc=1,
            device_id=(place // owners, lax.rem(place, owners)),
            device_id_type=MESH,
        )
        return carry

    lax.fori_loop(1, devices, greet, 0)

    loads = [
        pltpu.make_async_copy(out_weight, out_held, load_sem.at[0]),
        pltpu.make_async_copy(w_gate.at[0], gate_held, load_sem.at[1]),
        pltpu.make_async_copy(w_up.at[0], up_held, load_sem.at[2]),
        pltpu.make_async_copy(w_down.at[0], down_held, load_sem.at[3]),
    ]
    for load in loads:
        load.start()

    def send(source, target, send_sem, recv_sem, to_group, to_owner):
        pltpu.make_async_remote_copy(
            src_ref=source,
            dst_ref=target,
            send_sem=send_sem,
            recv_sem=recv_sem,
            device_id=(to_group, to_owner),
            device_id_type=MESH,
        ).start()

    def take(ref, sem):
        pltpu.make_async_copy(ref, ref, sem).wait()

    def fork_index(parent_group, child_group, pair):
        return (parent_group * held_groups + pair[0]) * fork_groups + (
            child_group * held_groups + pair[1]
        )

    for away in range(groups):
        target = lax.rem(group + away, groups)
        for slot, pair in enumerate(pairs):
            parent = lax.rem(fork_parent[fork_index(group, target, pair)], rows)
            chosen = kv_cache[parent]
            if away == 0:
                fork_recv[0, slot] = chosen
            else:
                fork_send[away, slot] = chosen
    pl.semaphore_wait(barrier, devices - 1)
    for away in range(1, groups):
        target = lax.rem(group + away, groups)
        send(
            fork_send.at[away],
            fork_recv.at[away],
            fork_send_sem.at[away],
            fork_recv_sem.at[away],
            target,
            owner,
        )

    shape = (rows, rows * positions_dev)
    row_at = lax.broadcasted_iota(jnp.int32, shape, 0)
    column_at = lax.broadcasted_iota(jnp.int32, shape, 1)
    length_at = jnp.zeros(shape, jnp.int32)
    for b in range(rows):
        length_at = jnp.where(row_at == b, lengths[b], length_at)
    position_at = owner * positions_dev + lax.rem(column_at, positions_dev)
    seen = (column_at // positions_dev == row_at) & (position_at < length_at)
    bias = jnp.where(seen, 0.0, HIDDEN_SCORE).astype(F32)
    bias = jnp.concatenate([bias] * grouping, axis=0)
    score_scale = 1.0 / math.sqrt(HD)
    own_query = query[:, pl.ds(pl.multiple_of(owner * HD, HD), HD)].astype(F32)
    own_kv = owner // grouping
    new_key = new_kv[:, pl.ds(pl.multiple_of(own_kv * HD, HD), HD)].astype(F32)
    new_value = new_kv[:, pl.ds(pl.multiple_of(key_width + own_kv * HD, HD), HD)].astype(F32)
    own_score = jnp.sum(own_query * new_key, axis=1, keepdims=True) * score_scale

    for away in range(1, groups):
        take(fork_recv.at[away], fork_recv_sem.at[away])
    for b in range(rows):
        kept = kv_cache[b].astype(F32)
        for away in range(groups):
            source = lax.rem(group + groups - away, groups)
            for slot, pair in enumerate(pairs):
                fork = fork_index(source, group, pair)
                hit = (fork_child[fork] - group * rows == b) & (owner >= fork_block[fork])
                kept = jnp.where(hit, fork_recv[away, slot].astype(F32), kept)
        cache[b] = kept.astype(BF16)

    lane = lax.broadcasted_iota(jnp.int32, (grouping * rows, HD), 1)
    for j in range(KVH):
        heads = [j * grouping + i for i in range(grouping)]
        grouped = jnp.concatenate([query[:, h * HD : (h + 1) * HD] for h in heads], axis=0)
        keys = cache[:, :, j * HD : (j + 1) * HD].reshape(rows * positions_dev, HD)
        values = cache[:, :, key_width + j * HD : key_width + (j + 1) * HD].reshape(
            rows * positions_dev, HD
        )
        scores = lax.dot_general(
            grouped, keys, (((1,), (1,)), ((), ())), preferred_element_type=F32
        )
        scores = scores * score_scale + bias
        peak = jnp.max(scores, axis=1, keepdims=True)
        weights = jnp.where(scores > 0.5 * HIDDEN_SCORE, jnp.exp(scores - peak), 0.0)
        total = jnp.sum(weights, axis=1, keepdims=True)
        part = jnp.dot(weights.astype(BF16), values, preferred_element_type=F32)
        peak_high = peak.astype(BF16).astype(F32)
        peak_mid = (peak - peak_high).astype(BF16).astype(F32)
        peak_low = peak - peak_high - peak_mid
        total_high = total.astype(BF16).astype(F32)
        total_low = total - total_high
        stats = jnp.where(lane == 0, peak_high, 0.0)
        stats = jnp.where(lane == 1, peak_mid, stats)
        stats = jnp.where(lane == 2, peak_low, stats)
        stats = jnp.where(lane == 3, total_high, stats)
        stats = jnp.where(lane == 4, total_low, stats)
        message = jnp.concatenate([part, stats], axis=1).astype(BF16)
        for i, h in enumerate(heads):
            part_send[h] = message[i * rows : (i + 1) * rows]

    def send_part(step, carry):
        target = lax.rem(owner + step, owners)
        send(
            part_send.at[target], part_recv.at[owner], part_sem.at[0], part_sem.at[1], group, target
        )
        return carry

    lax.fori_loop(1, owners, send_part, 0)
    part_recv[owner] = part_send[owner]
    picked = lax.broadcasted_iota(jnp.int32, (HD, 2 * HD), 0)
    side = lax.broadcasted_iota(jnp.int32, (HD, 2 * HD), 1) // HD
    spread = ((side == 0) & (picked < 3)) | ((side == 1) & ((picked == 3) | (picked == 4)))
    spread = jnp.where(spread, 1.0, 0.0).astype(BF16)
    take(part_recv.at[pl.ds(0, owners - 1)], part_sem.at[1])

    stats = part_recv[:, :, HD:].reshape(owners * rows, HD)
    stats = jnp.dot(stats, spread, preferred_element_type=F32).reshape(owners, rows, 2 * HD)
    peaks, totals = stats[:, :, :HD], stats[:, :, HD:]
    highest = jnp.maximum(jnp.max(peaks, axis=0), own_score)
    factors = jnp.exp(peaks - highest[None])
    own_weight = jnp.exp(own_score - highest)
    denominator = jnp.sum(totals * factors, axis=0) + own_weight
    attended = jnp.sum(part_recv[:, :, :HD].astype(F32) * factors, axis=0)
    attended = attended + own_weight.astype(BF16).astype(F32) * new_value
    attended = (attended / denominator).astype(BF16)

    loads[0].wait()
    tile = max(columns, 1024)
    blocks = tile // columns
    for k in range(width // tile):
        terms = jnp.dot(
            attended, out_held[:, k * tile : (k + 1) * tile], preferred_element_type=F32
        ).astype(BF16)
        for i in range(blocks):
            proj_send[k * blocks + i] = terms[:, i * columns : (i + 1) * columns]

    def send_proj(step, carry):
        target = lax.rem(owner + step, owners)
        send(
            proj_send.at[target], proj_recv.at[owner], proj_sem.at[0], proj_sem.at[1], group, target
        )
        return carry

    lax.fori_loop(1, owners, send_proj, 0)
    proj_recv[owner] = proj_send[owner]
    if slice_residual:
        start = pl.multiple_of(owner * columns, 128)
        own_residual = residual[:, pl.ds(start, columns)].astype(F32)
    else:
        own_residual = residual[...].astype(F32)
    take(proj_recv.at[pl.ds(0, owners - 1)], proj_sem.at[1])
    projected = jnp.sum(proj_recv[...].astype(F32), axis=0)
    attn_out[...] = projected.astype(BF16)
    own_rows = pl.ds(pl.multiple_of(group * rows, rows), rows)
    stream[owner, own_rows, :] = (own_residual + projected).astype(BF16)

    def send_stream(step, carry):
        target = lax.rem(owner + step, owners)
        for away in range(groups):
            to_group = lax.rem(group + away, groups)

            def go():
                send(
                    stream.at[owner, own_rows],
                    stream.at[owner, own_rows],
                    stream_send_sem,
                    stream_recv_sem.at[owner, group],
                    to_group,
                    target,
                )

            if away == 0:
                pl.when(step > 0)(go)
            else:
                go()
        return carry

    lax.fori_loop(0, owners, send_stream, 0)
    tokens = groups * rows
    lane_ids = route_ids[...]
    gates = jnp.sum(
        jnp.where(lane_ids == owner, route_weights[...], 0.0), axis=1, keepdims=True
    )
    loads[1].wait()
    loads[2].wait()
    inner = tile // columns
    units = gate_held.shape[1]

    def expand(step, state):
        gate_sum, up_sum, squares = state
        chunk = lax.rem(owner // inner + step, owners // inner)
        for i in range(inner):
            source = chunk * inner + i
            for g in range(groups):

                @pl.when((source != owner) | (g != group))
                def _():
                    take(
                        stream.at[source, pl.ds(g * rows, rows)], stream_recv_sem.at[source, g]
                    )

        x = jnp.concatenate([stream[chunk * inner + i] for i in range(inner)], axis=1)
        depth = pl.ds(pl.multiple_of(chunk * tile, tile), tile)
        gate_sum = gate_sum + jnp.dot(x, gate_held[depth, :], preferred_element_type=F32)
        up_sum = up_sum + jnp.dot(x, up_held[depth, :], preferred_element_type=F32)
        wide = x.astype(F32)
        return gate_sum, up_sum, squares + jnp.sum(wide * wide, axis=1, keepdims=True)

    zero = jnp.zeros((tokens, units), F32)
    gate_sum, up_sum, squares = lax.fori_loop(
        0, owners // inner, expand, (zero, zero, jnp.zeros((tokens, 1), F32))
    )
    inverse = lax.rsqrt(squares / width + 1e-06)
    gate_sum = gate_sum * inverse
    hidden = (gate_sum / (1.0 + jnp.exp(-gate_sum)) * (up_sum * inverse)).astype(BF16)

    loads[3].wait()
    place = group * owners + owner

    def contract(step, carry):
        chunk = lax.rem(owner // inner + step, owners // inner)
        span = pl.ds(pl.multiple_of(chunk * tile, tile), tile)
        terms = jnp.dot(hidden, down_held[:, span], preferred_element_type=F32)
        terms = (terms * gates).astype(BF16)
        for i in range(inner):
            target = chunk * inner + i
            for g in range(groups):
                slot = g * owners + target
                mix_send[slot] = terms[g * rows : (g + 1) * rows, i * columns : (i + 1) * columns]

                @pl.when(slot != place)
                def _():
                    send(
                        mix_send.at[slot],
                        mix_recv.at[place],
                        mix_sem.at[0],
                        mix_sem.at[1],
                        g,
                        target,
                    )

        return carry

    lax.fori_loop(0, owners // inner, contract, 0)
    mix_recv[place] = mix_send[place]
    take(mix_recv.at[pl.ds(0, devices - 1)], mix_sem.at[1])
    mix_out[...] = jnp.sum(mix_recv[...].astype(F32), axis=0).astype(BF16)

    for away in range(1, groups):
        take(fork_send.at[away], fork_send_sem.at[away])
    take(part_send.at[pl.ds(0, owners - 1)], part_sem.at[0])
    take(proj_send.at[pl.ds(0, owners - 1)], proj_sem.at[0])
    take(mix_send.at[pl.ds(0, devices - 1)], stream_send_sem)
    take(mix_send.at[pl.ds(0, devices - 1)], mix_sem.at[0])


def shards(
    query,
    new_kv,
    kv_cache,
    lengths,
    fork_parent,
    fork_child,
    fork_block,
    out_weight,
    residual,
    route_ids,
    route_weights,
    w_gate,
    w_up,
    w_down,
):
    groups = lax.axis_size("dp")
    owners = lax.axis_size("expert")
    devices = groups * owners
    rows, positions_dev, _ = kv_cache.shape
    heads = query.shape[1] // HD
    width = residual.shape[1]
    columns = width // owners
    slice_residual = columns % 128 == 0
    if not slice_residual:
        residual = lax.dynamic_slice_in_dim(
            residual, lax.axis_index("expert") * columns, columns, 1
        )
    fork_rows = (math.isqrt(fork_parent.shape[0]) // groups) ** 2
    fork_shape = (groups, fork_rows) + kv_cache.shape[1:]
    smem = pl.BlockSpec(memory_space=pltpu.SMEM)
    vmem = pl.BlockSpec(memory_space=pltpu.VMEM)
    anywhere = pl.BlockSpec(memory_space=pl.ANY)
    dma = pltpu.SemaphoreType.DMA
    block = jax.ShapeDtypeStruct((rows, columns), BF16)
    return pl.pallas_call(
        functools.partial(layer, groups, owners, slice_residual),
        out_shape=(block, block),
        in_specs=[smem] * 4 + [vmem] * 6 + [anywhere] * 4,
        out_specs=(vmem, vmem),
        scratch_shapes=[
            pltpu.VMEM(kv_cache.shape, BF16),
            pltpu.VMEM(out_weight.shape, BF16),
            pltpu.VMEM(w_gate.shape[1:], BF16),
            pltpu.VMEM(w_up.shape[1:], BF16),
            pltpu.VMEM(w_down.shape[1:], BF16),
            pltpu.VMEM(fork_shape, BF16),
            pltpu.VMEM(fork_shape, BF16),
            pltpu.VMEM((heads, rows, 2 * HD), BF16),
            pltpu.VMEM((owners, rows, 2 * HD), BF16),
            pltpu.VMEM((owners, rows, columns), BF16),
            pltpu.VMEM((owners, rows, columns), BF16),
            pltpu.VMEM((owners, groups * rows, columns), BF16),
            pltpu.VMEM((devices, rows, columns), BF16),
            pltpu.VMEM((devices, rows, columns), BF16),
            dma((4,)),
            dma((groups,)),
            dma((groups,)),
            dma((2,)),
            dma((2,)),
            dma,
            dma((owners, groups)),
            dma((2,)),
        ],
        compiler_params=pltpu.CompilerParams(
            collective_id=0, has_side_effects=True, vmem_limit_bytes=48 * 1024 * 1024
        ),
    )(
        lengths,
        fork_parent,
        fork_child,
        fork_block,
        query,
        new_kv,
        kv_cache,
        residual,
        route_ids,
        route_weights,
        out_weight,
        w_gate,
        w_up,
        w_down,
    )


def solution(mesh):
    in_specs = (
        P("dp", None),
        P("dp", None),
        P("dp", "expert", None),
        P("dp"),
        P(),
        P(),
        P(),
        P("expert", None),
        P("dp", None),
        P(),
        P(),
        P("expert", None, "dp"),
        P("expert", None, "dp"),
        P("expert", "dp", None),
    )
    out_specs = (P("dp", "expert"), P("dp", "expert"))
    return jax.shard_map(shards, mesh=mesh, in_specs=in_specs, out_specs=out_specs, check_vma=False)
```

```python
import functools
import math

import jax
import jax.numpy as jnp
from jax import lax
from jax.experimental import pallas as pl
from jax.experimental.pallas import tpu as pltpu
from jax.sharding import PartitionSpec as P

HD = 128
KVH = 4
MESH = pl.DeviceIdType.MESH
F32 = jnp.float32
BF16 = jnp.bfloat16
HIDDEN_SCORE = -1e30


def layer(
    groups,
    owners,
    slice_residual,
    lengths_in,
    fork_parent_in,
    fork_child_in,
    fork_block_in,
    query_in,
    new_kv_in,
    kv_cache_in,
    residual_in,
    route_ids_in,
    route_weights_in,
    out_weight,
    w_gate,
    w_up,
    w_down,
    attn_out,
    mix_out,
    lengths,
    fork_parent,
    fork_child,
    fork_block,
    query,
    new_kv,
    kv_cache,
    residual,
    route_ids,
    route_weights,
    out_held,
    gate_held,
    up_held,
    down_held,
    fork_send,
    fork_recv,
    part_send,
    part_recv,
    proj_send,
    proj_recv,
    stream,
    mix_send,
    mix_recv,
    load_sem,
    small_sem,
    fork_send_sem,
    fork_recv_sem,
    part_sem,
    proj_sem,
    stream_send_sem,
    stream_recv_sem,
    mix_sem,
):
    group = lax.axis_index("dp")
    owner = lax.axis_index("expert")
    devices = groups * owners
    rows = query.shape[0]
    positions_dev = kv_cache.shape[1]
    key_width = KVH * HD
    grouping = query.shape[1] // HD // KVH
    width = w_gate.shape[1]
    columns = width // owners
    fork_groups = math.isqrt(fork_parent.shape[0])
    held_groups = fork_groups // groups
    pairs = [(i, k) for i in range(held_groups) for k in range(held_groups)]

    barrier = pltpu.get_barrier_semaphore()

    def greet(step, carry):
        place = lax.rem(group * owners + owner + step, devices)
        pl.semaphore_signal(
            barrier,
            inc=1,
            device_id=(place // owners, lax.rem(place, owners)),
            device_id_type=MESH,
        )
        return carry

    start = pl.multiple_of(owner * columns, columns)
    wanted = residual_in.at[:, pl.ds(start, columns)] if slice_residual else residual_in
    small = [
        pltpu.make_async_copy(source, held, small_sem.at[i])
        for i, (source, held) in enumerate(
            [
                (fork_parent_in, fork_parent),
                (kv_cache_in, kv_cache),
                (fork_child_in, fork_child),
                (fork_block_in, fork_block),
                (lengths_in, lengths),
                (query_in, query),
                (new_kv_in, new_kv),
                (wanted, residual),
                (route_ids_in, route_ids),
                (route_weights_in, route_weights),
            ]
        )
    ]
    for load in small:
        load.start()
    lax.fori_loop(1, devices, greet, 0)

    loads = [
        pltpu.make_async_copy(out_weight, out_held, load_sem.at[0]),
        pltpu.make_async_copy(w_gate.at[0], gate_held, load_sem.at[1]),
        pltpu.make_async_copy(w_up.at[0], up_held, load_sem.at[2]),
        pltpu.make_async_copy(w_down.at[0], down_held, load_sem.at[3]),
    ]
    for load in loads:
        load.start()

    def send(source, target, send_sem, recv_sem, to_group, to_owner):
        pltpu.make_async_remote_copy(
            src_ref=source,
            dst_ref=target,
            send_sem=send_sem,
            recv_sem=recv_sem,
            device_id=(to_group, to_owner),
            device_id_type=MESH,
        ).start()

    def take(ref, sem):
        pltpu.make_async_copy(ref, ref, sem).wait()

    def fork_index(parent_group, child_group, pair):
        return (parent_group * held_groups + pair[0]) * fork_groups + (
            child_group * held_groups + pair[1]
        )

    small[0].wait()
    small[1].wait()
    for away in range(groups):
        target = lax.rem(group + away, groups)
        for slot, pair in enumerate(pairs):
            parent = lax.rem(fork_parent[fork_index(group, target, pair)], rows)
            chosen = kv_cache[parent]
            if away == 0:
                fork_recv[0, slot] = chosen
            else:
                fork_send[away, slot] = chosen
    for load in small[2:7]:
        load.wait()

    def row_lengths(shape):
        row_at = lax.broadcasted_iota(jnp.int32, shape, 0)
        length_at = jnp.zeros(shape, jnp.int32)
        for b in range(rows):
            length_at = jnp.where(row_at == b, lengths[b], length_at)
        column_at = lax.broadcasted_iota(jnp.int32, shape, 1)
        position_at = owner * positions_dev + lax.rem(column_at, positions_dev)
        return row_at, column_at // positions_dev, position_at < length_at

    def bias_of(seen):
        bias = jnp.where(seen, 0.0, HIDDEN_SCORE).astype(F32)
        return jnp.concatenate([bias] * grouping, axis=0)

    children = []
    for away in range(groups):
        source = lax.rem(group + groups - away, groups)
        for pair in pairs:
            fork = fork_index(source, group, pair)
            child = fork_child[fork] - group * rows
            children.append(jnp.where(owner >= fork_block[fork], child, -1))
    row_at, branch_at, seen = row_lengths((rows, rows * positions_dev))
    seen = seen & (branch_at == row_at)
    for child in children:
        seen = seen & (row_at != child)
    bias = bias_of(seen)
    row_at, fork_at, seen = row_lengths((rows, len(children) * positions_dev))
    child_at = jnp.full(row_at.shape, -1, jnp.int32)
    for i, child in enumerate(children):
        child_at = jnp.where(fork_at == i, child, child_at)
    fork_bias = bias_of(seen & (child_at == row_at))

    pl.semaphore_wait(barrier, devices - 1)
    for away in range(1, groups):
        target = lax.rem(group + away, groups)
        send(
            fork_send.at[away],
            fork_recv.at[away],
            fork_send_sem.at[away],
            fork_recv_sem.at[away],
            target,
            owner,
        )

    score_scale = 1.0 / math.sqrt(HD)

    def raw_scores(j, keys):
        heads = [j * grouping + i for i in range(grouping)]
        grouped = jnp.concatenate([query[:, h * HD : (h + 1) * HD] for h in heads], axis=0)
        scores = lax.dot_general(
            grouped, keys, (((1,), (1,)), ((), ())), preferred_element_type=F32
        )
        return scores * score_scale

    def head_rows(ref, at):
        return ref[..., at : at + HD].reshape(-1, HD)

    own_scores = [raw_scores(j, head_rows(kv_cache, j * HD)) + bias for j in range(KVH)]
    own_query = query[:, pl.ds(pl.multiple_of(owner * HD, HD), HD)].astype(F32)
    own_kv = owner // grouping
    new_key = new_kv[:, pl.ds(pl.multiple_of(own_kv * HD, HD), HD)].astype(F32)
    new_value = new_kv[:, pl.ds(pl.multiple_of(key_width + own_kv * HD, HD), HD)].astype(F32)
    own_score = jnp.sum(own_query * new_key, axis=1, keepdims=True) * score_scale
    for away in range(1, groups):
        take(fork_recv.at[away], fork_recv_sem.at[away])

    lane = lax.broadcasted_iota(jnp.int32, (grouping * rows, HD), 1)
    for j in range(KVH):
        heads = [j * grouping + i for i in range(grouping)]
        scores = own_scores[j]
        fork_scores = raw_scores(j, head_rows(fork_recv, j * HD)) + fork_bias
        peak = jnp.maximum(
            jnp.max(scores, axis=1, keepdims=True), jnp.max(fork_scores, axis=1, keepdims=True)
        )
        total = jnp.zeros_like(peak)
        part = jnp.zeros((grouping * rows, HD), F32)
        for some, held in ((scores, kv_cache), (fork_scores, fork_recv)):
            weights = jnp.where(some > 0.5 * HIDDEN_SCORE, jnp.exp(some - peak), 0.0)
            total = total + jnp.sum(weights, axis=1, keepdims=True)
            part = part + jnp.dot(
                weights.astype(BF16),
                head_rows(held, key_width + j * HD),
                preferred_element_type=F32,
            )
        peak_high = peak.astype(BF16).astype(F32)
        peak_mid = (peak - peak_high).astype(BF16).astype(F32)
        peak_low = peak - peak_high - peak_mid
        total_high = total.astype(BF16).astype(F32)
        total_low = total - total_high
        stats = jnp.where(lane == 0, peak_high, 0.0)
        stats = jnp.where(lane == 1, peak_mid, stats)
        stats = jnp.where(lane == 2, peak_low, stats)
        stats = jnp.where(lane == 3, total_high, stats)
        stats = jnp.where(lane == 4, total_low, stats)
        message = jnp.concatenate([part, stats], axis=1).astype(BF16)
        for i, h in enumerate(heads):
            part_send[h] = message[i * rows : (i + 1) * rows]

    def send_part(step, carry):
        target = lax.rem(owner + step, owners)
        send(
            part_send.at[target], part_recv.at[owner], part_sem.at[0], part_sem.at[1], group, target
        )
        return carry

    lax.fori_loop(1, owners, send_part, 0)
    part_recv[owner] = part_send[owner]
    picked = lax.broadcasted_iota(jnp.int32, (HD, 2 * HD), 0)
    side = lax.broadcasted_iota(jnp.int32, (HD, 2 * HD), 1) // HD
    spread = ((side == 0) & (picked < 3)) | ((side == 1) & ((picked == 3) | (picked == 4)))
    spread = jnp.where(spread, 1.0, 0.0).astype(BF16)
    take(part_recv.at[pl.ds(0, owners - 1)], part_sem.at[1])

    stats = part_recv[:, :, HD:].reshape(owners * rows, HD)
    stats = jnp.dot(stats, spread, preferred_element_type=F32).reshape(owners, rows, 2 * HD)
    peaks, totals = stats[:, :, :HD], stats[:, :, HD:]
    highest = jnp.maximum(jnp.max(peaks, axis=0), own_score)
    factors = jnp.exp(peaks - highest[None])
    own_weight = jnp.exp(own_score - highest)
    denominator = jnp.sum(totals * factors, axis=0) + own_weight
    attended = jnp.sum(part_recv[:, :, :HD].astype(F32) * factors, axis=0)
    attended = attended + own_weight.astype(BF16).astype(F32) * new_value
    attended = (attended / denominator).astype(BF16)

    loads[0].wait()
    tile = max(columns, 1024)
    blocks = tile // columns
    for k in range(width // tile):
        terms = jnp.dot(
            attended, out_held[:, k * tile : (k + 1) * tile], preferred_element_type=F32
        ).astype(BF16)
        for i in range(blocks):
            proj_send[k * blocks + i] = terms[:, i * columns : (i + 1) * columns]

    def send_proj(step, carry):
        target = lax.rem(owner + step, owners)
        send(
            proj_send.at[target], proj_recv.at[owner], proj_sem.at[0], proj_sem.at[1], group, target
        )
        return carry

    lax.fori_loop(1, owners, send_proj, 0)
    proj_recv[owner] = proj_send[owner]
    small[7].wait()
    own_residual = residual[...].astype(F32)
    take(proj_recv.at[pl.ds(0, owners - 1)], proj_sem.at[1])
    projected = jnp.sum(proj_recv[...].astype(F32), axis=0)
    attn_out[...] = projected.astype(BF16)
    own_rows = pl.ds(pl.multiple_of(group * rows, rows), rows)
    stream[owner, own_rows, :] = (own_residual + projected).astype(BF16)

    def send_stream(step, carry):
        target = lax.rem(owner + step, owners)
        for away in range(groups):
            to_group = lax.rem(group + away, groups)

            def go():
                send(
                    stream.at[owner, own_rows],
                    stream.at[owner, own_rows],
                    stream_send_sem,
                    stream_recv_sem.at[owner, group],
                    to_group,
                    target,
                )

            if away == 0:
                pl.when(step > 0)(go)
            else:
                go()
        return carry

    lax.fori_loop(0, owners, send_stream, 0)
    tokens = groups * rows
    small[8].wait()
    small[9].wait()
    gates = jnp.sum(
        jnp.where(route_ids[...] == owner, route_weights[...], 0.0), axis=0, keepdims=True
    )
    square = (tokens, tokens)
    diagonal = lax.broadcasted_iota(jnp.int32, square, 0) == lax.broadcasted_iota(
        jnp.int32, square, 1
    )
    gates = jnp.sum(
        jnp.where(diagonal, jnp.broadcast_to(gates, square), 0.0), axis=1, keepdims=True
    )
    loads[1].wait()
    loads[2].wait()
    inner = tile // columns
    units = gate_held.shape[1]

    def expand(step, state):
        gate_sum, up_sum, squares = state
        chunk = lax.rem(owner // inner + step, owners // inner)
        for i in range(inner):
            source = chunk * inner + i
            for g in range(groups):

                @pl.when((source != owner) | (g != group))
                def _():
                    take(
                        stream.at[source, pl.ds(g * rows, rows)], stream_recv_sem.at[source, g]
                    )

        x = jnp.concatenate([stream[chunk * inner + i] for i in range(inner)], axis=1)
        depth = pl.ds(pl.multiple_of(chunk * tile, tile), tile)
        gate_sum = gate_sum + jnp.dot(x, gate_held[depth, :], preferred_element_type=F32)
        up_sum = up_sum + jnp.dot(x, up_held[depth, :], preferred_element_type=F32)
        wide = x.astype(F32)
        return gate_sum, up_sum, squares + jnp.sum(wide * wide, axis=1, keepdims=True)

    zero = jnp.zeros((tokens, units), F32)
    gate_sum, up_sum, squares = lax.fori_loop(
        0, owners // inner, expand, (zero, zero, jnp.zeros((tokens, 1), F32))
    )
    inverse = lax.rsqrt(squares / width + 1e-06)
    gate_sum = gate_sum * inverse
    hidden = (gate_sum / (1.0 + jnp.exp(-gate_sum)) * (up_sum * inverse)).astype(BF16)

    loads[3].wait()
    place = group * owners + owner

    def contract(step, carry):
        chunk = lax.rem(owner // inner + step, owners // inner)
        span = pl.ds(pl.multiple_of(chunk * tile, tile), tile)
        terms = jnp.dot(hidden, down_held[:, span], preferred_element_type=F32)
        terms = (terms * gates).astype(BF16)
        for i in range(inner):
            target = chunk * inner + i
            for g in range(groups):
                slot = g * owners + target
                mix_send[slot] = terms[g * rows : (g + 1) * rows, i * columns : (i + 1) * columns]

                @pl.when(slot != place)
                def _():
                    send(
                        mix_send.at[slot],
                        mix_recv.at[place],
                        mix_sem.at[0],
                        mix_sem.at[1],
                        g,
                        target,
                    )

        return carry

    lax.fori_loop(0, owners // inner, contract, 0)
    mix_recv[place] = mix_send[place]
    take(mix_recv.at[pl.ds(0, devices - 1)], mix_sem.at[1])
    mix_out[...] = jnp.sum(mix_recv[...].astype(F32), axis=0).astype(BF16)

    for away in range(1, groups):
        take(fork_send.at[away], fork_send_sem.at[away])
    take(part_send.at[pl.ds(0, owners - 1)], part_sem.at[0])
    take(proj_send.at[pl.ds(0, owners - 1)], proj_sem.at[0])
    take(mix_send.at[pl.ds(0, devices - 1)], stream_send_sem)
    take(mix_send.at[pl.ds(0, devices - 1)], mix_sem.at[0])


def shards(
    query,
    new_kv,
    kv_cache,
    lengths,
    fork_parent,
    fork_child,
    fork_block,
    out_weight,
    residual,
    route_ids,
    route_weights,
    w_gate,
    w_up,
    w_down,
):
    groups = lax.axis_size("dp")
    owners = lax.axis_size("expert")
    devices = groups * owners
    rows, positions_dev, _ = kv_cache.shape
    heads = query.shape[1] // HD
    width = residual.shape[1]
    columns = width // owners
    slice_residual = columns % 128 == 0
    if not slice_residual:
        residual = lax.dynamic_slice_in_dim(
            residual, lax.axis_index("expert") * columns, columns, 1
        )
    fork_rows = (math.isqrt(fork_parent.shape[0]) // groups) ** 2
    fork_shape = (groups, fork_rows) + kv_cache.shape[1:]
    vmem = pl.BlockSpec(memory_space=pltpu.VMEM)
    far = pl.BlockSpec(memory_space=pltpu.HBM)
    dma = pltpu.SemaphoreType.DMA
    block = jax.ShapeDtypeStruct((rows, columns), BF16)
    return pl.pallas_call(
        functools.partial(layer, groups, owners, slice_residual),
        out_shape=(block, block),
        in_specs=[far] * 14,
        out_specs=(vmem, vmem),
        scratch_shapes=[
            pltpu.SMEM(lengths.shape, jnp.int32),
            pltpu.SMEM(fork_parent.shape, jnp.int32),
            pltpu.SMEM(fork_child.shape, jnp.int32),
            pltpu.SMEM(fork_block.shape, jnp.int32),
            pltpu.VMEM(query.shape, BF16),
            pltpu.VMEM(new_kv.shape, BF16),
            pltpu.VMEM(kv_cache.shape, BF16),
            pltpu.VMEM((rows, columns), BF16),
            pltpu.VMEM(route_ids.shape[::-1], jnp.int32),
            pltpu.VMEM(route_weights.shape[::-1], F32),
            pltpu.VMEM(out_weight.shape, BF16),
            pltpu.VMEM(w_gate.shape[1:], BF16),
            pltpu.VMEM(w_up.shape[1:], BF16),
            pltpu.VMEM(w_down.shape[1:], BF16),
            pltpu.VMEM(fork_shape, BF16),
            pltpu.VMEM(fork_shape, BF16),
            pltpu.VMEM((heads, rows, 2 * HD), BF16),
            pltpu.VMEM((owners, rows, 2 * HD), BF16),
            pltpu.VMEM((owners, rows, columns), BF16),
            pltpu.VMEM((owners, rows, columns), BF16),
            pltpu.VMEM((owners, groups * rows, columns), BF16),
            pltpu.VMEM((devices, rows, columns), BF16),
            pltpu.VMEM((devices, rows, columns), BF16),
            dma((4,)),
            dma((10,)),
            dma((groups,)),
            dma((groups,)),
            dma((2,)),
            dma((2,)),
            dma,
            dma((owners, groups)),
            dma((2,)),
        ],
        compiler_params=pltpu.CompilerParams(
            collective_id=0, has_side_effects=True, vmem_limit_bytes=64 * 1024 * 1024
        ),
    )(
        lengths,
        fork_parent,
        fork_child,
        fork_block,
        query,
        new_kv,
        kv_cache,
        residual,
        route_ids.T,
        route_weights.T,
        out_weight,
        w_gate,
        w_up,
        w_down,
    )


def solution(mesh):
    in_specs = (
        P("dp", None),
        P("dp", None),
        P("dp", "expert", None),
        P("dp"),
        P(),
        P(),
        P(),
        P("expert", None),
        P("dp", None),
        P(),
        P(),
        P("expert", None, "dp"),
        P("expert", None, "dp"),
        P("expert", "dp", None),
    )
    out_specs = (P("dp", "expert"), P("dp", "expert"))
    return jax.shard_map(shards, mesh=mesh, in_specs=in_specs, out_specs=out_specs, check_vma=False)
```

```python
import functools
import math

import jax
import jax.numpy as jnp
from jax import lax
from jax.experimental import pallas as pl
from jax.experimental.pallas import tpu as pltpu
from jax.sharding import PartitionSpec as P

HD = 128
KVH = 4
MESH = pl.DeviceIdType.MESH
F32 = jnp.float32
BF16 = jnp.bfloat16
HIDDEN_SCORE = -1e30


def layer(
    groups,
    owners,
    slice_residual,
    lengths_in,
    fork_parent_in,
    fork_child_in,
    fork_block_in,
    query_in,
    new_kv_in,
    kv_cache_in,
    residual_in,
    route_ids_in,
    route_weights_in,
    out_weight,
    w_gate,
    w_up,
    w_down,
    attn_out,
    mix_out,
    lengths,
    fork_parent,
    fork_child,
    fork_block,
    query,
    new_kv,
    kv_cache,
    residual,
    route_ids,
    route_weights,
    out_held,
    gate_held,
    up_held,
    down_held,
    fork_send,
    fork_recv,
    part_send,
    part_recv,
    proj_send,
    proj_recv,
    stream,
    mix_send,
    mix_pair,
    mix_sum,
    mix_recv,
    load_sem,
    small_sem,
    fork_send_sem,
    fork_recv_sem,
    part_sem,
    proj_sem,
    stream_sem,
    stream_recv_sem,
    relay_sem,
    pair_sem,
    mix_sem,
):
    group = lax.axis_index("dp")
    owner = lax.axis_index("expert")
    rows = query.shape[0]
    positions_dev = kv_cache.shape[1]
    key_width = KVH * HD
    grouping = query.shape[1] // HD // KVH
    width = w_gate.shape[1]
    columns = width // owners
    fork_groups = math.isqrt(fork_parent.shape[0])
    held_groups = fork_groups // groups
    pairs = [(i, k) for i in range(held_groups) for k in range(held_groups)]

    half = owners // 2
    core = lax.rem(owner, 2)
    chip = owner // 2
    sibling = owner + 1 - 2 * core

    def same_core(step):
        return 2 * lax.rem(chip + step, half) + core

    barrier = pltpu.get_barrier_semaphore()

    def greet(to_group, to_owner):
        pl.semaphore_signal(
            barrier, inc=1, device_id=(to_group, to_owner), device_id_type=MESH
        )

    def greet_group(step, carry):
        greet(group, lax.rem(owner + step, owners))
        return carry

    def greet_others(step, carry):
        for away in range(1, groups):
            greet(lax.rem(group + away, groups), same_core(step))
        return carry

    start = pl.multiple_of(owner * columns, columns)
    wanted = residual_in.at[:, pl.ds(start, columns)] if slice_residual else residual_in
    small = [
        pltpu.make_async_copy(source, held, small_sem.at[i])
        for i, (source, held) in enumerate(
            [
                (fork_parent_in, fork_parent),
                (kv_cache_in, kv_cache),
                (fork_child_in, fork_child),
                (fork_block_in, fork_block),
                (lengths_in, lengths),
                (query_in, query),
                (new_kv_in, new_kv),
                (wanted, residual),
                (route_ids_in, route_ids),
                (route_weights_in, route_weights),
            ]
        )
    ]
    for load in small:
        load.start()
    lax.fori_loop(1, owners, greet_group, 0)
    lax.fori_loop(0, half, greet_others, 0)

    loads = [
        pltpu.make_async_copy(out_weight, out_held, load_sem.at[0]),
        pltpu.make_async_copy(w_gate.at[0], gate_held, load_sem.at[1]),
        pltpu.make_async_copy(w_up.at[0], up_held, load_sem.at[2]),
        pltpu.make_async_copy(w_down.at[0], down_held, load_sem.at[3]),
    ]
    for load in loads:
        load.start()

    def send(source, target, send_sem, recv_sem, to_group, to_owner):
        pltpu.make_async_remote_copy(
            src_ref=source,
            dst_ref=target,
            send_sem=send_sem,
            recv_sem=recv_sem,
            device_id=(to_group, to_owner),
            device_id_type=MESH,
        ).start()

    def take(ref, sem):
        pltpu.make_async_copy(ref, ref, sem).wait()

    def fork_index(parent_group, child_group, pair):
        return (parent_group * held_groups + pair[0]) * fork_groups + (
            child_group * held_groups + pair[1]
        )

    small[0].wait()
    small[1].wait()
    for away in range(groups):
        target = lax.rem(group + away, groups)
        for slot, pair in enumerate(pairs):
            parent = lax.rem(fork_parent[fork_index(group, target, pair)], rows)
            chosen = kv_cache[parent]
            if away == 0:
                fork_recv[0, slot] = chosen
            else:
                fork_send[away, slot] = chosen
    for load in small[2:7]:
        load.wait()

    def row_lengths(shape):
        row_at = lax.broadcasted_iota(jnp.int32, shape, 0)
        length_at = jnp.zeros(shape, jnp.int32)
        for b in range(rows):
            length_at = jnp.where(row_at == b, lengths[b], length_at)
        column_at = lax.broadcasted_iota(jnp.int32, shape, 1)
        position_at = owner * positions_dev + lax.rem(column_at, positions_dev)
        return row_at, column_at // positions_dev, position_at < length_at

    def bias_of(seen):
        bias = jnp.where(seen, 0.0, HIDDEN_SCORE).astype(F32)
        return jnp.concatenate([bias] * grouping, axis=0)

    children = []
    for away in range(groups):
        source = lax.rem(group + groups - away, groups)
        for pair in pairs:
            fork = fork_index(source, group, pair)
            child = fork_child[fork] - group * rows
            children.append(jnp.where(owner >= fork_block[fork], child, -1))
    row_at, branch_at, seen = row_lengths((rows, rows * positions_dev))
    seen = seen & (branch_at == row_at)
    for child in children:
        seen = seen & (row_at != child)
    bias = bias_of(seen)
    row_at, fork_at, seen = row_lengths((rows, len(children) * positions_dev))
    child_at = jnp.full(row_at.shape, -1, jnp.int32)
    for i, child in enumerate(children):
        child_at = jnp.where(fork_at == i, child, child_at)
    fork_bias = bias_of(seen & (child_at == row_at))

    pl.semaphore_wait(barrier, owners - 1 + (groups - 1) * half)
    for away in range(1, groups):
        target = lax.rem(group + away, groups)
        send(
            fork_send.at[away],
            fork_recv.at[away],
            fork_send_sem.at[away],
            fork_recv_sem.at[away],
            target,
            owner,
        )

    score_scale = 1.0 / math.sqrt(HD)

    def raw_scores(j, keys):
        heads = [j * grouping + i for i in range(grouping)]
        grouped = jnp.concatenate([query[:, h * HD : (h + 1) * HD] for h in heads], axis=0)
        scores = lax.dot_general(
            grouped, keys, (((1,), (1,)), ((), ())), preferred_element_type=F32
        )
        return scores * score_scale

    def head_rows(ref, at):
        return ref[..., at : at + HD].reshape(-1, HD)

    own_scores = [raw_scores(j, head_rows(kv_cache, j * HD)) + bias for j in range(KVH)]
    own_query = query[:, pl.ds(pl.multiple_of(owner * HD, HD), HD)].astype(F32)
    own_kv = owner // grouping
    new_key = new_kv[:, pl.ds(pl.multiple_of(own_kv * HD, HD), HD)].astype(F32)
    new_value = new_kv[:, pl.ds(pl.multiple_of(key_width + own_kv * HD, HD), HD)].astype(F32)
    own_score = jnp.sum(own_query * new_key, axis=1, keepdims=True) * score_scale
    for away in range(1, groups):
        take(fork_recv.at[away], fork_recv_sem.at[away])

    lane = lax.broadcasted_iota(jnp.int32, (grouping * rows, HD), 1)
    for j in range(KVH):
        heads = [j * grouping + i for i in range(grouping)]
        scores = own_scores[j]
        fork_scores = raw_scores(j, head_rows(fork_recv, j * HD)) + fork_bias
        peak = jnp.maximum(
            jnp.max(scores, axis=1, keepdims=True), jnp.max(fork_scores, axis=1, keepdims=True)
        )
        total = jnp.zeros_like(peak)
        part = jnp.zeros((grouping * rows, HD), F32)
        for some, held in ((scores, kv_cache), (fork_scores, fork_recv)):
            weights = jnp.where(some > 0.5 * HIDDEN_SCORE, jnp.exp(some - peak), 0.0)
            total = total + jnp.sum(weights, axis=1, keepdims=True)
            part = part + jnp.dot(
                weights.astype(BF16),
                head_rows(held, key_width + j * HD),
                preferred_element_type=F32,
            )
        peak_high = peak.astype(BF16).astype(F32)
        peak_mid = (peak - peak_high).astype(BF16).astype(F32)
        peak_low = peak - peak_high - peak_mid
        total_high = total.astype(BF16).astype(F32)
        total_low = total - total_high
        stats = jnp.where(lane == 0, peak_high, 0.0)
        stats = jnp.where(lane == 1, peak_mid, stats)
        stats = jnp.where(lane == 2, peak_low, stats)
        stats = jnp.where(lane == 3, total_high, stats)
        stats = jnp.where(lane == 4, total_low, stats)
        message = jnp.concatenate([part, stats], axis=1).astype(BF16)
        for i, h in enumerate(heads):
            part_send[h] = message[i * rows : (i + 1) * rows]

    def send_part(step, carry):
        target = lax.rem(owner + step, owners)
        send(
            part_send.at[target], part_recv.at[owner], part_sem.at[0], part_sem.at[1], group, target
        )
        return carry

    lax.fori_loop(1, owners, send_part, 0)
    part_recv[owner] = part_send[owner]
    picked = lax.broadcasted_iota(jnp.int32, (HD, 2 * HD), 0)
    side = lax.broadcasted_iota(jnp.int32, (HD, 2 * HD), 1) // HD
    spread = ((side == 0) & (picked < 3)) | ((side == 1) & ((picked == 3) | (picked == 4)))
    spread = jnp.where(spread, 1.0, 0.0).astype(BF16)
    take(part_recv.at[pl.ds(0, owners - 1)], part_sem.at[1])

    stats = part_recv[:, :, HD:].reshape(owners * rows, HD)
    stats = jnp.dot(stats, spread, preferred_element_type=F32).reshape(owners, rows, 2 * HD)
    peaks, totals = stats[:, :, :HD], stats[:, :, HD:]
    highest = jnp.maximum(jnp.max(peaks, axis=0), own_score)
    factors = jnp.exp(peaks - highest[None])
    own_weight = jnp.exp(own_score - highest)
    denominator = jnp.sum(totals * factors, axis=0) + own_weight
    attended = jnp.sum(part_recv[:, :, :HD].astype(F32) * factors, axis=0)
    attended = attended + own_weight.astype(BF16).astype(F32) * new_value
    attended = (attended / denominator).astype(BF16)

    loads[0].wait()
    tile = max(columns, 1024)
    blocks = tile // columns
    for k in range(width // tile):
        terms = jnp.dot(
            attended, out_held[:, k * tile : (k + 1) * tile], preferred_element_type=F32
        ).astype(BF16)
        for i in range(blocks):
            proj_send[k * blocks + i] = terms[:, i * columns : (i + 1) * columns]

    def send_proj(step, carry):
        target = lax.rem(owner + step, owners)
        send(
            proj_send.at[target], proj_recv.at[owner], proj_sem.at[0], proj_sem.at[1], group, target
        )
        return carry

    lax.fori_loop(1, owners, send_proj, 0)
    proj_recv[owner] = proj_send[owner]
    small[7].wait()
    own_residual = residual[...].astype(F32)
    take(proj_recv.at[pl.ds(0, owners - 1)], proj_sem.at[1])
    projected = jnp.sum(proj_recv[...].astype(F32), axis=0)
    attn_out[...] = projected.astype(BF16)
    own_rows = pl.ds(pl.multiple_of(group * rows, rows), rows)
    stream[core, chip, own_rows, :] = (own_residual + projected).astype(BF16)

    def send_stream(step, carry):
        for away in range(groups):

            def go():
                send(
                    stream.at[core, chip, own_rows],
                    stream.at[core, chip, own_rows],
                    stream_sem.at[0],
                    stream_recv_sem.at[chip, group],
                    lax.rem(group + away, groups),
                    same_core(step),
                )

            if away == 0:
                pl.when(step > 0)(go)
            else:
                go()
        return carry

    lax.fori_loop(0, half, send_stream, 0)
    tokens = groups * rows
    small[8].wait()
    small[9].wait()
    gates = jnp.sum(
        jnp.where(route_ids[...] == owner, route_weights[...], 0.0), axis=0, keepdims=True
    )
    square = (tokens, tokens)
    diagonal = lax.broadcasted_iota(jnp.int32, square, 0) == lax.broadcasted_iota(
        jnp.int32, square, 1
    )
    gates = jnp.sum(
        jnp.where(diagonal, jnp.broadcast_to(gates, square), 0.0), axis=1, keepdims=True
    )
    loads[1].wait()
    loads[2].wait()
    chunks = width // tile
    inner = tile // columns // 2
    units = gate_held.shape[1]

    def expand(side, chunk, state):
        gate_sum, up_sum, squares = state
        for i in range(inner):
            block = chunk * inner + i
            x = stream[side, block]
            depth = pl.ds(pl.multiple_of((2 * block + side) * columns, columns), columns)
            gate_sum = gate_sum + jnp.dot(x, gate_held[depth, :], preferred_element_type=F32)
            up_sum = up_sum + jnp.dot(x, up_held[depth, :], preferred_element_type=F32)
            wide = x.astype(F32)
            squares = squares + jnp.sum(wide * wide, axis=1, keepdims=True)
        return gate_sum, up_sum, squares

    def chunk_at(step):
        return lax.rem(chip // inner + step, chunks)

    def expand_arrived(step, state):
        chunk = chunk_at(step)
        for i in range(inner):
            block = chunk * inner + i
            for g in range(groups):

                @pl.when((block != chip) | (g != group))
                def _():
                    take(
                        stream.at[core, block, pl.ds(g * rows, rows)],
                        stream_recv_sem.at[block, g],
                    )

        relayed = stream.at[core, pl.ds(chunk * inner, inner)]
        send(relayed, relayed, stream_sem.at[1], relay_sem.at[chunk], group, sibling)
        return expand(core, chunk, state)

    def expand_relayed(step, state):
        chunk = chunk_at(step)
        take(stream.at[1 - core, pl.ds(chunk * inner, inner)], relay_sem.at[chunk])
        return expand(1 - core, chunk, state)

    zero = jnp.zeros((tokens, units), F32)
    state = (zero, zero, jnp.zeros((tokens, 1), F32))
    state = lax.fori_loop(0, chunks, expand_arrived, state)
    gate_sum, up_sum, squares = lax.fori_loop(0, chunks, expand_relayed, state)
    inverse = lax.rsqrt(squares / width + 1e-06)
    gate_sum = gate_sum * inverse
    hidden = (gate_sum / (1.0 + jnp.exp(-gate_sum)) * (up_sum * inverse)).astype(BF16)

    loads[3].wait()
    place = group * half + chip

    def contract(step):
        chunk = chunk_at(step)
        span = pl.ds(pl.multiple_of(chunk * tile, tile), tile)
        terms = jnp.dot(hidden, down_held[:, span], preferred_element_type=F32)
        terms = (terms * gates).astype(BF16)
        for i in range(inner):
            for side in range(2):
                at = (2 * i + side) * columns
                for g in range(groups):
                    mix_send[side, chunk * inner + i, g] = terms[
                        g * rows : (g + 1) * rows, at : at + columns
                    ]
        some = pl.ds(chunk * inner, inner)
        send(
            mix_send.at[1 - core, some],
            mix_pair.at[some],
            mix_sem.at[0],
            pair_sem.at[chunk],
            group,
            sibling,
        )

    def spread_sums(step):
        chunk = chunk_at(step)
        some = pl.ds(chunk * inner, inner)
        take(mix_pair.at[some], pair_sem.at[chunk])
        mix_sum[some] = (mix_send[core, some].astype(F32) + mix_pair[some].astype(F32)).astype(
            BF16
        )
        for i in range(inner):
            block = chunk * inner + i
            for g in range(groups):

                @pl.when((block != chip) | (g != group))
                def _():
                    send(
                        mix_sum.at[block, g],
                        mix_recv.at[place],
                        mix_sem.at[1],
                        mix_sem.at[2],
                        g,
                        2 * block + core,
                    )

    for step in range(chunks):
        contract(step)
        if step > 0:
            spread_sums(step - 1)
    spread_sums(chunks - 1)
    mix_recv[place] = mix_sum[chip, group]
    others = pl.ds(0, half * groups - 1)
    take(mix_recv.at[others], mix_sem.at[2])
    mix_out[...] = jnp.sum(mix_recv[...].astype(F32), axis=0).astype(BF16)

    for away in range(1, groups):
        take(fork_send.at[away], fork_send_sem.at[away])
    take(part_send.at[pl.ds(0, owners - 1)], part_sem.at[0])
    take(proj_send.at[pl.ds(0, owners - 1)], proj_sem.at[0])
    take(mix_recv.at[others], stream_sem.at[0])
    take(stream.at[0], stream_sem.at[1])
    take(mix_pair, mix_sem.at[0])
    take(mix_recv.at[others], mix_sem.at[1])


def shards(
    query,
    new_kv,
    kv_cache,
    lengths,
    fork_parent,
    fork_child,
    fork_block,
    out_weight,
    residual,
    route_ids,
    route_weights,
    w_gate,
    w_up,
    w_down,
):
    groups = lax.axis_size("dp")
    owners = lax.axis_size("expert")
    half = owners // 2
    rows, positions_dev, _ = kv_cache.shape
    heads = query.shape[1] // HD
    width = residual.shape[1]
    columns = width // owners
    chunks = width // max(columns, 1024)
    slice_residual = columns % 128 == 0
    if not slice_residual:
        residual = lax.dynamic_slice_in_dim(
            residual, lax.axis_index("expert") * columns, columns, 1
        )
    fork_rows = (math.isqrt(fork_parent.shape[0]) // groups) ** 2
    fork_shape = (groups, fork_rows) + kv_cache.shape[1:]
    vmem = pl.BlockSpec(memory_space=pltpu.VMEM)
    far = pl.BlockSpec(memory_space=pltpu.HBM)
    dma = pltpu.SemaphoreType.DMA
    block = jax.ShapeDtypeStruct((rows, columns), BF16)
    return pl.pallas_call(
        functools.partial(layer, groups, owners, slice_residual),
        out_shape=(block, block),
        in_specs=[far] * 14,
        out_specs=(vmem, vmem),
        scratch_shapes=[
            pltpu.SMEM(lengths.shape, jnp.int32),
            pltpu.SMEM(fork_parent.shape, jnp.int32),
            pltpu.SMEM(fork_child.shape, jnp.int32),
            pltpu.SMEM(fork_block.shape, jnp.int32),
            pltpu.VMEM(query.shape, BF16),
            pltpu.VMEM(new_kv.shape, BF16),
            pltpu.VMEM(kv_cache.shape, BF16),
            pltpu.VMEM((rows, columns), BF16),
            pltpu.VMEM(route_ids.shape[::-1], jnp.int32),
            pltpu.VMEM(route_weights.shape[::-1], F32),
            pltpu.VMEM(out_weight.shape, BF16),
            pltpu.VMEM(w_gate.shape[1:], BF16),
            pltpu.VMEM(w_up.shape[1:], BF16),
            pltpu.VMEM(w_down.shape[1:], BF16),
            pltpu.VMEM(fork_shape, BF16),
            pltpu.VMEM(fork_shape, BF16),
            pltpu.VMEM((heads, rows, 2 * HD), BF16),
            pltpu.VMEM((owners, rows, 2 * HD), BF16),
            pltpu.VMEM((owners, rows, columns), BF16),
            pltpu.VMEM((owners, rows, columns), BF16),
            pltpu.VMEM((2, half, groups * rows, columns), BF16),
            pltpu.VMEM((2, half, groups, rows, columns), BF16),
            pltpu.VMEM((half, groups, rows, columns), BF16),
            pltpu.VMEM((half, groups, rows, columns), BF16),
            pltpu.VMEM((half * groups, rows, columns), BF16),
            dma((4,)),
            dma((10,)),
            dma((groups,)),
            dma((groups,)),
            dma((2,)),
            dma((2,)),
            dma((2,)),
            dma((half, groups)),
            dma((chunks,)),
            dma((chunks,)),
            dma((3,)),
        ],
        compiler_params=pltpu.CompilerParams(
            collective_id=0, has_side_effects=True, vmem_limit_bytes=64 * 1024 * 1024
        ),
    )(
        lengths,
        fork_parent,
        fork_child,
        fork_block,
        query,
        new_kv,
        kv_cache,
        residual,
        route_ids.T,
        route_weights.T,
        out_weight,
        w_gate,
        w_up,
        w_down,
    )


def solution(mesh):
    in_specs = (
        P("dp", None),
        P("dp", None),
        P("dp", "expert", None),
        P("dp"),
        P(),
        P(),
        P(),
        P("expert", None),
        P("dp", None),
        P(),
        P(),
        P("expert", None, "dp"),
        P("expert", None, "dp"),
        P("expert", "dp", None),
    )
    out_specs = (P("dp", "expert"), P("dp", "expert"))
    return jax.shard_map(shards, mesh=mesh, in_specs=in_specs, out_specs=out_specs, check_vma=False)
```

```python
import functools
import math

import jax
import jax.numpy as jnp
from jax import lax
from jax.experimental import pallas as pl
from jax.experimental.pallas import tpu as pltpu
from jax.sharding import PartitionSpec as P

HD = 128
KVH = 4
MESH = pl.DeviceIdType.MESH
F32 = jnp.float32
BF16 = jnp.bfloat16
HIDDEN_SCORE = -1e30


def layer(
    groups,
    owners,
    slice_residual,
    lengths_in,
    fork_parent_in,
    fork_child_in,
    fork_block_in,
    query_in,
    new_kv_in,
    kv_cache_in,
    residual_in,
    route_ids_in,
    route_weights_in,
    out_weight,
    w_gate,
    w_up,
    w_down,
    outs,
    lengths,
    fork_parent,
    fork_child,
    fork_block,
    query,
    new_kv,
    kv_cache,
    residual,
    route_ids,
    route_weights,
    out_held,
    gate_held,
    up_held,
    down_held,
    fork_send,
    fork_recv,
    part_send,
    part_recv,
    proj_send,
    proj_recv,
    stream,
    mix_send,
    mix_pair,
    mix_sum,
    mix_recv,
    load_sem,
    small_sem,
    fork_send_sem,
    fork_recv_sem,
    part_sem,
    proj_sem,
    stream_sem,
    stream_recv_sem,
    relay_sem,
    pair_sem,
    mix_sem,
):
    group = lax.axis_index("dp")
    owner = lax.axis_index("expert")
    rows = query.shape[0]
    positions_dev = kv_cache.shape[1]
    key_width = KVH * HD
    grouping = query.shape[1] // HD // KVH
    width = w_gate.shape[1]
    columns = width // owners
    fork_groups = math.isqrt(fork_parent.shape[0])
    held_groups = fork_groups // groups
    pairs = [(i, k) for i in range(held_groups) for k in range(held_groups)]

    half = owners // 2
    core = lax.rem(owner, 2)
    chip = owner // 2
    sibling = owner + 1 - 2 * core

    def same_core(step):
        return 2 * lax.rem(chip + step, half) + core

    barrier = pltpu.get_barrier_semaphore()

    def greet(to_group, to_owner):
        pl.semaphore_signal(
            barrier, inc=1, device_id=(to_group, to_owner), device_id_type=MESH
        )

    def greet_group(step, carry):
        greet(group, lax.rem(owner + step, owners))
        return carry

    def greet_others(step, carry):
        for away in range(1, groups):
            greet(lax.rem(group + away, groups), same_core(step))
        return carry

    start = pl.multiple_of(owner * columns, columns)
    wanted = residual_in.at[:, pl.ds(start, columns)] if slice_residual else residual_in
    small = [
        pltpu.make_async_copy(source, held, small_sem.at[i])
        for i, (source, held) in enumerate(
            [
                (fork_parent_in, fork_parent),
                (kv_cache_in, kv_cache),
                (fork_child_in, fork_child),
                (fork_block_in, fork_block),
                (lengths_in, lengths),
                (query_in, query),
                (new_kv_in, new_kv),
                (wanted, residual),
                (route_ids_in, route_ids),
                (route_weights_in, route_weights),
            ]
        )
    ]
    for load in small:
        load.start()
    lax.fori_loop(1, owners, greet_group, 0)
    lax.fori_loop(0, half, greet_others, 0)

    loads = [
        pltpu.make_async_copy(out_weight, out_held, load_sem.at[0]),
        pltpu.make_async_copy(w_gate.at[0], gate_held, load_sem.at[1]),
        pltpu.make_async_copy(w_up.at[0], up_held, load_sem.at[2]),
        pltpu.make_async_copy(w_down.at[0], down_held, load_sem.at[3]),
    ]
    for load in loads:
        load.start()

    def send(source, target, send_sem, recv_sem, to_group, to_owner):
        pltpu.make_async_remote_copy(
            src_ref=source,
            dst_ref=target,
            send_sem=send_sem,
            recv_sem=recv_sem,
            device_id=(to_group, to_owner),
            device_id_type=MESH,
        ).start()

    def take(ref, sem):
        pltpu.make_async_copy(ref, ref, sem).wait()

    def fork_index(parent_group, child_group, pair):
        return (parent_group * held_groups + pair[0]) * fork_groups + (
            child_group * held_groups + pair[1]
        )

    small[0].wait()
    small[1].wait()
    for away in range(groups):
        target = lax.rem(group + away, groups)
        for slot, pair in enumerate(pairs):
            parent = lax.rem(fork_parent[fork_index(group, target, pair)], rows)
            chosen = kv_cache[parent]
            if away == 0:
                fork_recv[0, slot] = chosen
            else:
                fork_send[away, slot] = chosen
    for load in small[2:7]:
        load.wait()

    def row_lengths(shape):
        row_at = lax.broadcasted_iota(jnp.int32, shape, 0)
        length_at = jnp.zeros(shape, jnp.int32)
        for b in range(rows):
            length_at = jnp.where(row_at == b, lengths[b], length_at)
        column_at = lax.broadcasted_iota(jnp.int32, shape, 1)
        position_at = owner * positions_dev + lax.rem(column_at, positions_dev)
        return row_at, column_at // positions_dev, position_at < length_at

    def bias_of(seen):
        bias = jnp.where(seen, 0.0, HIDDEN_SCORE).astype(F32)
        return jnp.concatenate([bias] * grouping, axis=0)

    children = []
    for away in range(groups):
        source = lax.rem(group + groups - away, groups)
        for pair in pairs:
            fork = fork_index(source, group, pair)
            child = fork_child[fork] - group * rows
            children.append(jnp.where(owner >= fork_block[fork], child, -1))
    row_at, branch_at, seen = row_lengths((rows, rows * positions_dev))
    seen = seen & (branch_at == row_at)
    for child in children:
        seen = seen & (row_at != child)
    bias = bias_of(seen)
    row_at, fork_at, seen = row_lengths((rows, len(children) * positions_dev))
    child_at = jnp.full(row_at.shape, -1, jnp.int32)
    for i, child in enumerate(children):
        child_at = jnp.where(fork_at == i, child, child_at)
    fork_bias = bias_of(seen & (child_at == row_at))

    pl.semaphore_wait(barrier, owners - 1 + (groups - 1) * half)
    for away in range(1, groups):
        target = lax.rem(group + away, groups)
        send(
            fork_send.at[away],
            fork_recv.at[away],
            fork_send_sem.at[away],
            fork_recv_sem.at[away],
            target,
            owner,
        )

    score_scale = 1.0 / math.sqrt(HD)

    def raw_scores(j, keys):
        heads = [j * grouping + i for i in range(grouping)]
        grouped = jnp.concatenate([query[:, h * HD : (h + 1) * HD] for h in heads], axis=0)
        scores = lax.dot_general(
            grouped, keys, (((1,), (1,)), ((), ())), preferred_element_type=F32
        )
        return scores * score_scale

    def head_rows(ref, at):
        return ref[..., at : at + HD].reshape(-1, HD)

    own_scores = [raw_scores(j, head_rows(kv_cache, j * HD)) + bias for j in range(KVH)]
    own_query = query[:, pl.ds(pl.multiple_of(owner * HD, HD), HD)].astype(F32)
    own_kv = owner // grouping
    new_key = new_kv[:, pl.ds(pl.multiple_of(own_kv * HD, HD), HD)].astype(F32)
    new_value = new_kv[:, pl.ds(pl.multiple_of(key_width + own_kv * HD, HD), HD)].astype(F32)
    own_score = jnp.sum(own_query * new_key, axis=1, keepdims=True) * score_scale
    for away in range(1, groups):
        take(fork_recv.at[away], fork_recv_sem.at[away])

    lane = lax.broadcasted_iota(jnp.int32, (grouping * rows, HD), 1)
    for j in range(KVH):
        heads = [j * grouping + i for i in range(grouping)]
        scores = own_scores[j]
        fork_scores = raw_scores(j, head_rows(fork_recv, j * HD)) + fork_bias
        peak = jnp.maximum(
            jnp.max(scores, axis=1, keepdims=True), jnp.max(fork_scores, axis=1, keepdims=True)
        )
        total = jnp.zeros_like(peak)
        part = jnp.zeros((grouping * rows, HD), F32)
        for some, held in ((scores, kv_cache), (fork_scores, fork_recv)):
            weights = jnp.where(some > 0.5 * HIDDEN_SCORE, jnp.exp(some - peak), 0.0)
            total = total + jnp.sum(weights, axis=1, keepdims=True)
            part = part + jnp.dot(
                weights.astype(BF16),
                head_rows(held, key_width + j * HD),
                preferred_element_type=F32,
            )
        peak_high = peak.astype(BF16).astype(F32)
        peak_mid = (peak - peak_high).astype(BF16).astype(F32)
        peak_low = peak - peak_high - peak_mid
        total_high = total.astype(BF16).astype(F32)
        total_low = total - total_high
        stats = jnp.where(lane == 0, peak_high, 0.0)
        stats = jnp.where(lane == 1, peak_mid, stats)
        stats = jnp.where(lane == 2, peak_low, stats)
        stats = jnp.where(lane == 3, total_high, stats)
        stats = jnp.where(lane == 4, total_low, stats)
        message = jnp.concatenate([part, stats], axis=1).astype(BF16)
        for i, h in enumerate(heads):
            part_send[h] = message[i * rows : (i + 1) * rows]

    def send_part(step, carry):
        target = lax.rem(owner + step, owners)
        send(
            part_send.at[target], part_recv.at[owner], part_sem.at[0], part_sem.at[1], group, target
        )
        return carry

    lax.fori_loop(1, owners, send_part, 0)
    part_recv[owner] = part_send[owner]
    picked = lax.broadcasted_iota(jnp.int32, (HD, 2 * HD), 0)
    side = lax.broadcasted_iota(jnp.int32, (HD, 2 * HD), 1) // HD
    spread = ((side == 0) & (picked < 3)) | ((side == 1) & ((picked == 3) | (picked == 4)))
    spread = jnp.where(spread, 1.0, 0.0).astype(BF16)
    take(part_recv.at[pl.ds(0, owners - 1)], part_sem.at[1])

    stats = part_recv[:, :, HD:].reshape(owners * rows, HD)
    stats = jnp.dot(stats, spread, preferred_element_type=F32).reshape(owners, rows, 2 * HD)
    peaks, totals = stats[:, :, :HD], stats[:, :, HD:]
    highest = jnp.maximum(jnp.max(peaks, axis=0), own_score)
    factors = jnp.exp(peaks - highest[None])
    own_weight = jnp.exp(own_score - highest)
    denominator = jnp.sum(totals * factors, axis=0) + own_weight
    attended = jnp.sum(part_recv[:, :, :HD].astype(F32) * factors, axis=0)
    attended = attended + own_weight.astype(BF16).astype(F32) * new_value
    attended = (attended / denominator).astype(BF16)

    loads[0].wait()
    tile = max(columns, 1024)
    blocks = tile // columns
    for k in range(width // tile):
        terms = jnp.dot(
            attended, out_held[:, k * tile : (k + 1) * tile], preferred_element_type=F32
        ).astype(BF16)
        for i in range(blocks):
            proj_send[k * blocks + i] = terms[:, i * columns : (i + 1) * columns]

    def send_proj(step, carry):
        target = lax.rem(owner + step, owners)
        send(
            proj_send.at[target], proj_recv.at[owner], proj_sem.at[0], proj_sem.at[1], group, target
        )
        return carry

    lax.fori_loop(1, owners, send_proj, 0)
    proj_recv[owner] = proj_send[owner]
    small[7].wait()
    own_residual = residual[...].astype(F32)
    take(proj_recv.at[pl.ds(0, owners - 1)], proj_sem.at[1])
    projected = jnp.sum(proj_recv[...].astype(F32), axis=0)
    outs[0] = projected.astype(BF16)
    own_rows = pl.ds(pl.multiple_of(group * rows, rows), rows)
    stream[core, chip, own_rows, :] = (own_residual + projected).astype(BF16)

    def send_stream(step, carry):
        for away in range(groups):

            def go():
                send(
                    stream.at[core, chip, own_rows],
                    stream.at[core, chip, own_rows],
                    stream_sem.at[0],
                    stream_recv_sem.at[chip, group],
                    lax.rem(group + away, groups),
                    same_core(step),
                )

            if away == 0:
                pl.when(step > 0)(go)
            else:
                go()
        return carry

    lax.fori_loop(0, half, send_stream, 0)
    tokens = groups * rows
    small[8].wait()
    small[9].wait()
    gates = jnp.sum(
        jnp.where(route_ids[...] == owner, route_weights[...], 0.0), axis=0, keepdims=True
    )
    square = (tokens, tokens)
    diagonal = lax.broadcasted_iota(jnp.int32, square, 0) == lax.broadcasted_iota(
        jnp.int32, square, 1
    )
    gates = jnp.sum(
        jnp.where(diagonal, jnp.broadcast_to(gates, square), 0.0), axis=1, keepdims=True
    )
    loads[1].wait()
    loads[2].wait()
    chunks = width // tile
    inner = tile // columns // 2
    units = gate_held.shape[1]

    def expand(side, chunk, state):
        gate_sum, up_sum, squares = state
        for i in range(inner):
            block = chunk * inner + i
            x = stream[side, block]
            depth = pl.ds(pl.multiple_of((2 * block + side) * columns, columns), columns)
            gate_sum = gate_sum + jnp.dot(x, gate_held[depth, :], preferred_element_type=F32)
            up_sum = up_sum + jnp.dot(x, up_held[depth, :], preferred_element_type=F32)
            wide = x.astype(F32)
            squares = squares + jnp.sum(wide * wide, axis=1, keepdims=True)
        return gate_sum, up_sum, squares

    def chunk_at(step):
        return lax.rem(chip // inner + step, chunks)

    def expand_arrived(step, state):
        chunk = chunk_at(step)
        for i in range(inner):
            block = chunk * inner + i
            for g in range(groups):

                @pl.when((block != chip) | (g != group))
                def _():
                    take(
                        stream.at[core, block, pl.ds(g * rows, rows)],
                        stream_recv_sem.at[block, g],
                    )

        relayed = stream.at[core, pl.ds(chunk * inner, inner)]
        send(relayed, relayed, stream_sem.at[1], relay_sem.at[chunk], group, sibling)
        return expand(core, chunk, state)

    zero = jnp.zeros((tokens, units), F32)
    state = (zero, zero, jnp.zeros((tokens, 1), F32))
    state = lax.fori_loop(0, chunks, expand_arrived, state)
    for chunk in range(chunks):
        take(stream.at[1 - core, pl.ds(chunk * inner, inner)], relay_sem.at[chunk])
    for chunk in range(chunks):
        state = expand(1 - core, chunk, state)
    gate_sum, up_sum, squares = state
    inverse = lax.rsqrt(squares / width + 1e-06)
    gate_sum = gate_sum * inverse
    hidden = (gate_sum / (1.0 + jnp.exp(-gate_sum)) * (up_sum * inverse)).astype(BF16)

    loads[3].wait()
    place = group * half + chip

    def contract(step):
        chunk = chunk_at(step)
        span = pl.ds(pl.multiple_of(chunk * tile, tile), tile)
        terms = jnp.dot(hidden, down_held[:, span], preferred_element_type=F32)
        terms = (terms * gates).astype(BF16)
        for i in range(inner):
            for side in range(2):
                at = (2 * i + side) * columns
                for g in range(groups):
                    mix_send[side, chunk * inner + i, g] = terms[
                        g * rows : (g + 1) * rows, at : at + columns
                    ]
        some = pl.ds(chunk * inner, inner)
        send(
            mix_send.at[1 - core, some],
            mix_pair.at[some],
            mix_sem.at[0],
            pair_sem.at[chunk],
            group,
            sibling,
        )

    def spread_sums(step):
        chunk = chunk_at(step)
        some = pl.ds(chunk * inner, inner)
        take(mix_pair.at[some], pair_sem.at[chunk])
        mix_sum[some] = (mix_send[core, some].astype(F32) + mix_pair[some].astype(F32)).astype(
            BF16
        )
        for i in range(inner):
            block = chunk * inner + i
            for g in range(groups):

                @pl.when((block != chip) | (g != group))
                def _():
                    send(
                        mix_sum.at[block, g],
                        mix_recv.at[place],
                        mix_sem.at[1],
                        mix_sem.at[2],
                        g,
                        2 * block + core,
                    )

    for step in range(chunks):
        contract(step)
        if step > 0:
            spread_sums(step - 1)
    spread_sums(chunks - 1)
    mix_recv[place] = mix_sum[chip, group]
    others = pl.ds(0, half * groups - 1)
    take(mix_recv.at[others], mix_sem.at[2])
    outs[1] = jnp.sum(mix_recv[...].astype(F32), axis=0).astype(BF16)

    for away in range(1, groups):
        take(fork_send.at[away], fork_send_sem.at[away])
    take(part_send.at[pl.ds(0, owners - 1)], part_sem.at[0])
    take(proj_send.at[pl.ds(0, owners - 1)], proj_sem.at[0])
    take(mix_recv.at[others], stream_sem.at[0])
    take(stream.at[0], stream_sem.at[1])
    take(mix_pair, mix_sem.at[0])
    take(mix_recv.at[others], mix_sem.at[1])


def shards(
    query,
    new_kv,
    kv_cache,
    lengths,
    fork_parent,
    fork_child,
    fork_block,
    out_weight,
    residual,
    route_ids,
    route_weights,
    w_gate,
    w_up,
    w_down,
):
    groups = lax.axis_size("dp")
    owners = lax.axis_size("expert")
    half = owners // 2
    rows, positions_dev, _ = kv_cache.shape
    heads = query.shape[1] // HD
    width = residual.shape[1]
    columns = width // owners
    chunks = width // max(columns, 1024)
    slice_residual = columns % 128 == 0
    if not slice_residual:
        residual = lax.dynamic_slice_in_dim(
            residual, lax.axis_index("expert") * columns, columns, 1
        )
    fork_rows = (math.isqrt(fork_parent.shape[0]) // groups) ** 2
    fork_shape = (groups, fork_rows) + kv_cache.shape[1:]
    vmem = pl.BlockSpec(memory_space=pltpu.VMEM)
    far = pl.BlockSpec(memory_space=pltpu.HBM)
    dma = pltpu.SemaphoreType.DMA
    both = pl.pallas_call(
        functools.partial(layer, groups, owners, slice_residual),
        out_shape=jax.ShapeDtypeStruct((2, rows, columns), BF16),
        in_specs=[far] * 14,
        out_specs=vmem,
        scratch_shapes=[
            pltpu.SMEM(lengths.shape, jnp.int32),
            pltpu.SMEM(fork_parent.shape, jnp.int32),
            pltpu.SMEM(fork_child.shape, jnp.int32),
            pltpu.SMEM(fork_block.shape, jnp.int32),
            pltpu.VMEM(query.shape, BF16),
            pltpu.VMEM(new_kv.shape, BF16),
            pltpu.VMEM(kv_cache.shape, BF16),
            pltpu.VMEM((rows, columns), BF16),
            pltpu.VMEM(route_ids.shape[::-1], jnp.int32),
            pltpu.VMEM(route_weights.shape[::-1], F32),
            pltpu.VMEM(out_weight.shape, BF16),
            pltpu.VMEM(w_gate.shape[1:], BF16),
            pltpu.VMEM(w_up.shape[1:], BF16),
            pltpu.VMEM(w_down.shape[1:], BF16),
            pltpu.VMEM(fork_shape, BF16),
            pltpu.VMEM(fork_shape, BF16),
            pltpu.VMEM((heads, rows, 2 * HD), BF16),
            pltpu.VMEM((owners, rows, 2 * HD), BF16),
            pltpu.VMEM((owners, rows, columns), BF16),
            pltpu.VMEM((owners, rows, columns), BF16),
            pltpu.VMEM((2, half, groups * rows, columns), BF16),
            pltpu.VMEM((2, half, groups, rows, columns), BF16),
            pltpu.VMEM((half, groups, rows, columns), BF16),
            pltpu.VMEM((half, groups, rows, columns), BF16),
            pltpu.VMEM((half * groups, rows, columns), BF16),
            dma((4,)),
            dma((10,)),
            dma((groups,)),
            dma((groups,)),
            dma((2,)),
            dma((2,)),
            dma((2,)),
            dma((half, groups)),
            dma((chunks,)),
            dma((chunks,)),
            dma((3,)),
        ],
        compiler_params=pltpu.CompilerParams(
            collective_id=0, has_side_effects=True, vmem_limit_bytes=64 * 1024 * 1024
        ),
    )(
        lengths,
        fork_parent,
        fork_child,
        fork_block,
        query,
        new_kv,
        kv_cache,
        residual,
        route_ids.T,
        route_weights.T,
        out_weight,
        w_gate,
        w_up,
        w_down,
    )
    return both[0], both[1]


def solution(mesh):
    in_specs = (
        P("dp", None),
        P("dp", None),
        P("dp", "expert", None),
        P("dp"),
        P(),
        P(),
        P(),
        P("expert", None),
        P("dp", None),
        P(),
        P(),
        P("expert", None, "dp"),
        P("expert", None, "dp"),
        P("expert", "dp", None),
    )
    out_specs = (P("dp", "expert"), P("dp", "expert"))
    return jax.shard_map(shards, mesh=mesh, in_specs=in_specs, out_specs=out_specs, check_vma=False)
```

```python
import functools
import math

import jax
import jax.numpy as jnp
from jax import lax
from jax.experimental import pallas as pl
from jax.experimental.pallas import tpu as pltpu
from jax.sharding import PartitionSpec as P

HD = 128
KVH = 4
MESH = pl.DeviceIdType.MESH
F32 = jnp.float32
BF16 = jnp.bfloat16
HIDDEN_SCORE = -1e30


def layer(
    groups,
    owners,
    slice_residual,
    lengths_in,
    fork_parent_in,
    fork_child_in,
    fork_block_in,
    query_in,
    new_kv_in,
    kv_cache_in,
    residual_in,
    route_ids_in,
    route_weights_in,
    out_weight,
    w_gate,
    w_up,
    w_down,
    outs,
    lengths,
    fork_parent,
    fork_child,
    fork_block,
    query,
    new_kv,
    kv_cache,
    residual,
    route_ids,
    route_weights,
    out_held,
    gate_held,
    up_held,
    down_held,
    fork_send,
    fork_recv,
    part_send,
    part_recv,
    proj_send,
    proj_recv,
    stream,
    mix_send,
    mix_pair,
    mix_sum,
    mix_recv,
    load_sem,
    small_sem,
    fork_send_sem,
    fork_recv_sem,
    part_sem,
    proj_sem,
    stream_sem,
    stream_recv_sem,
    relay_sem,
    pair_sem,
    mix_sem,
):
    group = lax.axis_index("dp")
    owner = lax.axis_index("expert")
    rows = query.shape[0]
    positions_dev = kv_cache.shape[1]
    key_width = KVH * HD
    grouping = query.shape[1] // HD // KVH
    width = w_gate.shape[1]
    columns = width // owners
    fork_groups = math.isqrt(fork_parent.shape[0])
    held_groups = fork_groups // groups
    pairs = [(i, k) for i in range(held_groups) for k in range(held_groups)]

    half = owners // 2
    core = lax.rem(owner, 2)
    chip = owner // 2
    sibling = owner + 1 - 2 * core

    def same_core(step):
        return 2 * lax.rem(chip + step, half) + core

    barrier = pltpu.get_barrier_semaphore()

    def greet(to_group, to_owner):
        pl.semaphore_signal(
            barrier, inc=1, device_id=(to_group, to_owner), device_id_type=MESH
        )

    def greet_group(step, carry):
        greet(group, lax.rem(owner + step, owners))
        return carry

    def greet_others(step, carry):
        for away in range(1, groups):
            greet(lax.rem(group + away, groups), same_core(step))
        return carry

    start = pl.multiple_of(owner * columns, columns)
    wanted = residual_in.at[:, pl.ds(start, columns)] if slice_residual else residual_in
    small = [
        pltpu.make_async_copy(source, held, small_sem.at[i])
        for i, (source, held) in enumerate(
            [
                (fork_parent_in, fork_parent),
                (kv_cache_in, kv_cache),
                (fork_child_in, fork_child),
                (fork_block_in, fork_block),
                (lengths_in, lengths),
                (query_in, query),
                (new_kv_in, new_kv),
                (wanted, residual),
                (route_ids_in, route_ids),
                (route_weights_in, route_weights),
            ]
        )
    ]
    for load in small:
        load.start()
    lax.fori_loop(1, owners, greet_group, 0)
    lax.fori_loop(0, half, greet_others, 0)

    loads = [
        pltpu.make_async_copy(out_weight, out_held, load_sem.at[0]),
        pltpu.make_async_copy(w_gate.at[0], gate_held, load_sem.at[1]),
        pltpu.make_async_copy(w_up.at[0], up_held, load_sem.at[2]),
        pltpu.make_async_copy(w_down.at[0], down_held, load_sem.at[3]),
    ]
    for load in loads:
        load.start()

    def send(source, target, send_sem, recv_sem, to_group, to_owner):
        pltpu.make_async_remote_copy(
            src_ref=source,
            dst_ref=target,
            send_sem=send_sem,
            recv_sem=recv_sem,
            device_id=(to_group, to_owner),
            device_id_type=MESH,
        ).start()

    def take(ref, sem):
        pltpu.make_async_copy(ref, ref, sem).wait()

    def fork_index(parent_group, child_group, pair):
        return (parent_group * held_groups + pair[0]) * fork_groups + (
            child_group * held_groups + pair[1]
        )

    small[0].wait()
    small[1].wait()
    for away in range(groups):
        target = lax.rem(group + away, groups)
        for slot, pair in enumerate(pairs):
            parent = lax.rem(fork_parent[fork_index(group, target, pair)], rows)
            chosen = kv_cache[parent]
            if away == 0:
                fork_recv[0, slot] = chosen
            else:
                fork_send[away, slot] = chosen
    for load in small[2:7]:
        load.wait()

    def row_lengths(shape):
        row_at = lax.broadcasted_iota(jnp.int32, shape, 0)
        length_at = jnp.zeros(shape, jnp.int32)
        for b in range(rows):
            length_at = jnp.where(row_at == b, lengths[b], length_at)
        column_at = lax.broadcasted_iota(jnp.int32, shape, 1)
        position_at = owner * positions_dev + lax.rem(column_at, positions_dev)
        return row_at, column_at // positions_dev, position_at < length_at

    def bias_of(seen):
        bias = jnp.where(seen, 0.0, HIDDEN_SCORE).astype(F32)
        return jnp.concatenate([bias] * grouping, axis=0)

    children = []
    for away in range(groups):
        source = lax.rem(group + groups - away, groups)
        for pair in pairs:
            fork = fork_index(source, group, pair)
            child = fork_child[fork] - group * rows
            children.append(jnp.where(owner >= fork_block[fork], child, -1))
    row_at, branch_at, seen = row_lengths((rows, rows * positions_dev))
    seen = seen & (branch_at == row_at)
    for child in children:
        seen = seen & (row_at != child)
    bias = bias_of(seen)
    row_at, fork_at, seen = row_lengths((rows, len(children) * positions_dev))
    child_at = jnp.full(row_at.shape, -1, jnp.int32)
    for i, child in enumerate(children):
        child_at = jnp.where(fork_at == i, child, child_at)
    fork_bias = bias_of(seen & (child_at == row_at))

    pl.semaphore_wait(barrier, owners - 1 + (groups - 1) * half)
    for away in range(1, groups):
        target = lax.rem(group + away, groups)
        send(
            fork_send.at[away],
            fork_recv.at[away],
            fork_send_sem.at[away],
            fork_recv_sem.at[away],
            target,
            owner,
        )

    score_scale = 1.0 / math.sqrt(HD)

    def raw_scores(j, keys):
        heads = [j * grouping + i for i in range(grouping)]
        grouped = jnp.concatenate([query[:, h * HD : (h + 1) * HD] for h in heads], axis=0)
        scores = lax.dot_general(
            grouped, keys, (((1,), (1,)), ((), ())), preferred_element_type=F32
        )
        return scores * score_scale

    def head_rows(ref, at):
        return ref[..., at : at + HD].reshape(-1, HD)

    own_scores = [raw_scores(j, head_rows(kv_cache, j * HD)) + bias for j in range(KVH)]
    own_query = query[:, pl.ds(pl.multiple_of(owner * HD, HD), HD)].astype(F32)
    own_kv = owner // grouping
    new_key = new_kv[:, pl.ds(pl.multiple_of(own_kv * HD, HD), HD)].astype(F32)
    new_value = new_kv[:, pl.ds(pl.multiple_of(key_width + own_kv * HD, HD), HD)].astype(F32)
    own_score = jnp.sum(own_query * new_key, axis=1, keepdims=True) * score_scale
    for away in range(1, groups):
        take(fork_recv.at[away], fork_recv_sem.at[away])

    lane = lax.broadcasted_iota(jnp.int32, (grouping * rows, HD), 1)
    for j in range(KVH):
        heads = [j * grouping + i for i in range(grouping)]
        scores = own_scores[j]
        fork_scores = raw_scores(j, head_rows(fork_recv, j * HD)) + fork_bias
        peak = jnp.maximum(
            jnp.max(scores, axis=1, keepdims=True), jnp.max(fork_scores, axis=1, keepdims=True)
        )
        total = jnp.zeros_like(peak)
        part = jnp.zeros((grouping * rows, HD), F32)
        for some, held in ((scores, kv_cache), (fork_scores, fork_recv)):
            weights = jnp.where(some > 0.5 * HIDDEN_SCORE, jnp.exp(some - peak), 0.0)
            total = total + jnp.sum(weights, axis=1, keepdims=True)
            part = part + jnp.dot(
                weights.astype(BF16),
                head_rows(held, key_width + j * HD),
                preferred_element_type=F32,
            )
        peak_high = peak.astype(BF16).astype(F32)
        peak_mid = (peak - peak_high).astype(BF16).astype(F32)
        peak_low = peak - peak_high - peak_mid
        total_high = total.astype(BF16).astype(F32)
        total_low = total - total_high
        stats = jnp.where(lane == 0, peak_high, 0.0)
        stats = jnp.where(lane == 1, peak_mid, stats)
        stats = jnp.where(lane == 2, peak_low, stats)
        stats = jnp.where(lane == 3, total_high, stats)
        stats = jnp.where(lane == 4, total_low, stats)
        message = jnp.concatenate([part, stats], axis=1).astype(BF16)
        for i, h in enumerate(heads):
            part_send[h] = message[i * rows : (i + 1) * rows]

    def send_part(step, carry):
        target = lax.rem(owner + step, owners)
        send(
            part_send.at[target], part_recv.at[owner], part_sem.at[0], part_sem.at[1], group, target
        )
        return carry

    lax.fori_loop(1, owners, send_part, 0)
    part_recv[owner] = part_send[owner]
    picked = lax.broadcasted_iota(jnp.int32, (HD, 2 * HD), 0)
    side = lax.broadcasted_iota(jnp.int32, (HD, 2 * HD), 1) // HD
    spread = ((side == 0) & (picked < 3)) | ((side == 1) & ((picked == 3) | (picked == 4)))
    spread = jnp.where(spread, 1.0, 0.0).astype(BF16)
    take(part_recv.at[pl.ds(0, owners - 1)], part_sem.at[1])

    stats = part_recv[:, :, HD:].reshape(owners * rows, HD)
    stats = jnp.dot(stats, spread, preferred_element_type=F32).reshape(owners, rows, 2 * HD)
    peaks, totals = stats[:, :, :HD], stats[:, :, HD:]
    highest = jnp.maximum(jnp.max(peaks, axis=0), own_score)
    factors = jnp.exp(peaks - highest[None])
    own_weight = jnp.exp(own_score - highest)
    denominator = jnp.sum(totals * factors, axis=0) + own_weight
    attended = jnp.sum(part_recv[:, :, :HD].astype(F32) * factors, axis=0)
    attended = attended + own_weight.astype(BF16).astype(F32) * new_value
    attended = (attended / denominator).astype(BF16)

    loads[0].wait()
    tile = max(columns, 1024)
    blocks = tile // columns
    for step in range(width // tile):
        chunk = lax.rem(owner // blocks + step + 1, width // tile)
        span = pl.ds(pl.multiple_of(chunk * tile, tile), tile)
        terms = jnp.dot(attended, out_held[:, span], preferred_element_type=F32).astype(BF16)
        for i in range(blocks):
            target = chunk * blocks + i
            proj_send[target] = terms[:, i * columns : (i + 1) * columns]

            @pl.when(target != owner)
            def _():
                send(
                    proj_send.at[target],
                    proj_recv.at[owner],
                    proj_sem.at[0],
                    proj_sem.at[1],
                    group,
                    target,
                )

    proj_recv[owner] = proj_send[owner]
    small[7].wait()
    own_residual = residual[...].astype(F32)
    take(proj_recv.at[pl.ds(0, owners - 1)], proj_sem.at[1])
    projected = jnp.sum(proj_recv[...].astype(F32), axis=0)
    outs[0] = projected.astype(BF16)
    own_rows = pl.ds(pl.multiple_of(group * rows, rows), rows)
    stream[core, chip, own_rows, :] = (own_residual + projected).astype(BF16)

    def send_stream(step, carry):
        for away in range(groups):

            def go():
                send(
                    stream.at[core, chip, own_rows],
                    stream.at[core, chip, own_rows],
                    stream_sem.at[0],
                    stream_recv_sem.at[chip, group],
                    lax.rem(group + away, groups),
                    same_core(step),
                )

            if away == 0:
                pl.when(step > 0)(go)
            else:
                go()
        return carry

    lax.fori_loop(0, half, send_stream, 0)
    tokens = groups * rows
    small[8].wait()
    small[9].wait()
    gates = jnp.sum(
        jnp.where(route_ids[...] == owner, route_weights[...], 0.0), axis=0, keepdims=True
    )
    square = (tokens, tokens)
    diagonal = lax.broadcasted_iota(jnp.int32, square, 0) == lax.broadcasted_iota(
        jnp.int32, square, 1
    )
    gates = jnp.sum(
        jnp.where(diagonal, jnp.broadcast_to(gates, square), 0.0), axis=1, keepdims=True
    )
    loads[1].wait()
    loads[2].wait()
    chunks = width // tile
    inner = tile // columns // 2
    units = gate_held.shape[1]

    def expand(side, chunk, state):
        gate_sum, up_sum, squares = state
        for i in range(inner):
            block = chunk * inner + i
            x = stream[side, block]
            depth = pl.ds(pl.multiple_of((2 * block + side) * columns, columns), columns)
            gate_sum = gate_sum + jnp.dot(x, gate_held[depth, :], preferred_element_type=F32)
            up_sum = up_sum + jnp.dot(x, up_held[depth, :], preferred_element_type=F32)
            wide = x.astype(F32)
            squares = squares + jnp.sum(wide * wide, axis=1, keepdims=True)
        return gate_sum, up_sum, squares

    def chunk_at(step):
        return lax.rem(chip // inner + step, chunks)

    def expand_arrived(step, state):
        chunk = chunk_at(step)
        for i in range(inner):
            block = chunk * inner + i
            for g in range(groups):

                @pl.when((block != chip) | (g != group))
                def _():
                    take(
                        stream.at[core, block, pl.ds(g * rows, rows)],
                        stream_recv_sem.at[block, g],
                    )

        relayed = stream.at[core, pl.ds(chunk * inner, inner)]
        send(relayed, relayed, stream_sem.at[1], relay_sem.at[chunk], group, sibling)
        return expand(core, chunk, state)

    zero = jnp.zeros((tokens, units), F32)
    state = (zero, zero, jnp.zeros((tokens, 1), F32))
    state = lax.fori_loop(0, chunks, expand_arrived, state)
    for chunk in range(chunks):
        take(stream.at[1 - core, pl.ds(chunk * inner, inner)], relay_sem.at[chunk])
    for chunk in range(chunks):
        state = expand(1 - core, chunk, state)
    gate_sum, up_sum, squares = state
    inverse = lax.rsqrt(squares / width + 1e-06)
    gate_sum = gate_sum * inverse
    hidden = (gate_sum / (1.0 + jnp.exp(-gate_sum)) * (up_sum * inverse)).astype(BF16)

    loads[3].wait()
    place = group * half + chip

    def contract(step):
        chunk = chunk_at(step + 1)
        span = pl.ds(pl.multiple_of(chunk * tile, tile), tile)
        terms = jnp.dot(hidden, down_held[:, span], preferred_element_type=F32)
        terms = (terms * gates).astype(BF16)
        for i in range(inner):
            for side in range(2):
                at = (2 * i + side) * columns
                for g in range(groups):
                    mix_send[side, chunk * inner + i, g] = terms[
                        g * rows : (g + 1) * rows, at : at + columns
                    ]
        some = pl.ds(chunk * inner, inner)
        send(
            mix_send.at[1 - core, some],
            mix_pair.at[some],
            mix_sem.at[0],
            pair_sem.at[chunk],
            group,
            sibling,
        )

    def spread_sums(step):
        chunk = chunk_at(step + 1)
        some = pl.ds(chunk * inner, inner)
        take(mix_pair.at[some], pair_sem.at[chunk])
        mix_sum[some] = (mix_send[core, some].astype(F32) + mix_pair[some].astype(F32)).astype(
            BF16
        )
        for i in range(inner):
            block = chunk * inner + i
            for g in range(groups):

                @pl.when((block != chip) | (g != group))
                def _():
                    send(
                        mix_sum.at[block, g],
                        mix_recv.at[place],
                        mix_sem.at[1],
                        mix_sem.at[2],
                        g,
                        2 * block + core,
                    )

    for step in range(chunks):
        contract(step)
        if step > 0:
            spread_sums(step - 1)
    spread_sums(chunks - 1)
    mix_recv[place] = mix_sum[chip, group]
    others = pl.ds(0, half * groups - 1)
    take(mix_recv.at[others], mix_sem.at[2])
    outs[1] = jnp.sum(mix_recv[...].astype(F32), axis=0).astype(BF16)

    for away in range(1, groups):
        take(fork_send.at[away], fork_send_sem.at[away])
    take(part_send.at[pl.ds(0, owners - 1)], part_sem.at[0])
    take(proj_send.at[pl.ds(0, owners - 1)], proj_sem.at[0])
    take(mix_recv.at[others], stream_sem.at[0])
    take(stream.at[0], stream_sem.at[1])
    take(mix_pair, mix_sem.at[0])
    take(mix_recv.at[others], mix_sem.at[1])


def shards(
    query,
    new_kv,
    kv_cache,
    lengths,
    fork_parent,
    fork_child,
    fork_block,
    out_weight,
    residual,
    route_ids,
    route_weights,
    w_gate,
    w_up,
    w_down,
):
    groups = lax.axis_size("dp")
    owners = lax.axis_size("expert")
    half = owners // 2
    rows, positions_dev, _ = kv_cache.shape
    heads = query.shape[1] // HD
    width = residual.shape[1]
    columns = width // owners
    chunks = width // max(columns, 1024)
    slice_residual = columns % 128 == 0
    if not slice_residual:
        residual = lax.dynamic_slice_in_dim(
            residual, lax.axis_index("expert") * columns, columns, 1
        )
    fork_rows = (math.isqrt(fork_parent.shape[0]) // groups) ** 2
    fork_shape = (groups, fork_rows) + kv_cache.shape[1:]
    vmem = pl.BlockSpec(memory_space=pltpu.VMEM)
    far = pl.BlockSpec(memory_space=pltpu.HBM)
    dma = pltpu.SemaphoreType.DMA
    both = pl.pallas_call(
        functools.partial(layer, groups, owners, slice_residual),
        out_shape=jax.ShapeDtypeStruct((2, rows, columns), BF16),
        in_specs=[far] * 14,
        out_specs=vmem,
        scratch_shapes=[
            pltpu.SMEM(lengths.shape, jnp.int32),
            pltpu.SMEM(fork_parent.shape, jnp.int32),
            pltpu.SMEM(fork_child.shape, jnp.int32),
            pltpu.SMEM(fork_block.shape, jnp.int32),
            pltpu.VMEM(query.shape, BF16),
            pltpu.VMEM(new_kv.shape, BF16),
            pltpu.VMEM(kv_cache.shape, BF16),
            pltpu.VMEM((rows, columns), BF16),
            pltpu.VMEM(route_ids.shape[::-1], jnp.int32),
            pltpu.VMEM(route_weights.shape[::-1], F32),
            pltpu.VMEM(out_weight.shape, BF16),
            pltpu.VMEM(w_gate.shape[1:], BF16),
            pltpu.VMEM(w_up.shape[1:], BF16),
            pltpu.VMEM(w_down.shape[1:], BF16),
            pltpu.VMEM(fork_shape, BF16),
            pltpu.VMEM(fork_shape, BF16),
            pltpu.VMEM((heads, rows, 2 * HD), BF16),
            pltpu.VMEM((owners, rows, 2 * HD), BF16),
            pltpu.VMEM((owners, rows, columns), BF16),
            pltpu.VMEM((owners, rows, columns), BF16),
            pltpu.VMEM((2, half, groups * rows, columns), BF16),
            pltpu.VMEM((2, half, groups, rows, columns), BF16),
            pltpu.VMEM((half, groups, rows, columns), BF16),
            pltpu.VMEM((half, groups, rows, columns), BF16),
            pltpu.VMEM((half * groups, rows, columns), BF16),
            dma((4,)),
            dma((10,)),
            dma((groups,)),
            dma((groups,)),
            dma((2,)),
            dma((2,)),
            dma((2,)),
            dma((half, groups)),
            dma((chunks,)),
            dma((chunks,)),
            dma((3,)),
        ],
        compiler_params=pltpu.CompilerParams(
            collective_id=0, has_side_effects=True, vmem_limit_bytes=64 * 1024 * 1024
        ),
    )(
        lengths,
        fork_parent,
        fork_child,
        fork_block,
        query,
        new_kv,
        kv_cache,
        residual,
        route_ids.T,
        route_weights.T,
        out_weight,
        w_gate,
        w_up,
        w_down,
    )
    return both[0], both[1]


def solution(mesh):
    in_specs = (
        P("dp", None),
        P("dp", None),
        P("dp", "expert", None),
        P("dp"),
        P(),
        P(),
        P(),
        P("expert", None),
        P("dp", None),
        P(),
        P(),
        P("expert", None, "dp"),
        P("expert", None, "dp"),
        P("expert", "dp", None),
    )
    out_specs = (P("dp", "expert"), P("dp", "expert"))
    return jax.shard_map(shards, mesh=mesh, in_specs=in_specs, out_specs=out_specs, check_vma=False)
```
